32 devices in a mesh: grp: 2 (over x), tok: 16 (over z, y, core).
Axes of the slice: x: 2, y: 2, z: 4, core: 2. Of those that a mesh axis runs over, the one named last changes fastest.
Arguments:
- keys: bfloat16 [4096, 1024], P(('grp', 'tok')), parts along dimension 0, may hold values from -6 to 6
- values: bfloat16 [4096, 1024], P(('grp', 'tok')), parts along dimension 0, may hold values from -6 to 6
- queries: bfloat16 [4096, 1024], P(('grp', 'tok')), parts along dimension 0, may hold values from -6 to 6
- rates: float32 [2, 4096], P(None, ('grp', 'tok')), parts along dimension 1, may hold values from 0.3 to 3
- fast_weights: bfloat16 [2, 3, 512, 512], replicated, may hold values from -0.25 to 0.25
Outputs:
- readout: bfloat16 [4096, 1024], P(('grp', 'tok')), parts along dimension 0
- new_weights: bfloat16 [4, 3, 512, 512], P('grp'), parts along dimension 0
The draws below stay inside these ranges and needn't reach their ends.
There are 2 independent parts, one for each index of `grp`. The reference program is written for one: setup_inputs(seed, part) draws one part's arguments, and reference() takes and returns one part's arrays. A program takes and returns all parts, laid end to end along the dimension named above; an argument that names none is the same for every part. Nothing has to cross between parts.
All inputs are finite; a program needn't handle non-finite values.
Results may differ from the reference program's by a relative error of at most 0.017.
Values may be sent and summed in bfloat16 or wider, within the bound.
No kernel may reach another device: no remote copies, remote signals or barrier semaphores. Data moves between devices by JAX's collectives and lax.ppermute only.
A program may use at most 64 MiB of HBM per device.

```python
import jax
import jax.numpy as jnp
from jax import lax

DH = 512
HEADS = 2
NS_STEPS = 2
GROUP = 2048


def draw_rates(key, part):
    ramp = 1.0 + 2.0 * jnp.arange(GROUP, dtype=jnp.float32) / (GROUP - 1)
    base = jnp.exp(jax.random.uniform(key, (HEADS, GROUP), jnp.float32, jnp.log(0.3), 0.0))
    return jnp.clip(base * ramp[None, :], 0.3, 3.0)


def levels(own_key, shape, shards, low, largest):
    factor_of = 1.0
    for axis_at, blocks in shards:
        draws = jax.random.uniform(jax.random.fold_in(jax.random.fold_in(own_key, 6), axis_at), (blocks,), jnp.float32, low / len(shards), largest / len(shards))
        factor_of = factor_of * jnp.repeat(jnp.exp(draws), shape[axis_at] // blocks).reshape((-1,) + (1,) * (len(shape) - 1 - axis_at))
    return factor_of


def scatter_about(stream_key, shape, scale, reach, cuts=(), held_as=jnp.bfloat16):
    values = jax.random.normal(stream_key, shape, jnp.float32) * scale
    if len(cuts) > 0:
        values = levels(stream_key, shape, cuts, -0.22, 0.18) * values
    return jnp.clip(values, min=-reach, max=reach).astype(held_as)


def setup_inputs(seed: int = 0, part: int = 0) -> dict:
    arg_keys = jax.random.split(jax.random.key(seed), 6)
    own_keys = jax.random.split(jax.random.fold_in(arg_keys[5], part), 6)
    return {
        "keys": scatter_about(own_keys[0], (GROUP, HEADS * DH), 1.0, 6.0, ((0, 16),)),
        "values": scatter_about(own_keys[1], (GROUP, HEADS * DH), 1.0, 6.0, ((0, 16),)),
        "queries": scatter_about(own_keys[2], (GROUP, HEADS * DH), 1.0, 6.0, ((0, 16),)),
        "rates": draw_rates(jax.random.fold_in(jax.random.fold_in(arg_keys[5], part), 71), part),
        "fast_weights": scatter_about(arg_keys[4], (HEADS, 3, DH, DH), DH ** -0.5, 0.25),
    }


def swiglu_grads(key_rows, value_rows, rate_col, gate_w, up_w, down_w):
    gate = jnp.dot(key_rows, gate_w, preferred_element_type=jnp.float32)
    upper = jnp.dot(key_rows, up_w, preferred_element_type=jnp.float32)
    sigma = jax.nn.sigmoid(gate)
    silu_gate = gate * sigma
    hidden = (silu_gate * upper).astype(jnp.bfloat16)
    outer = (-rate_col[:, None] * value_rows.astype(jnp.float32)).astype(jnp.bfloat16)
    back = jnp.dot(outer, down_w.T, preferred_element_type=jnp.float32)
    d_gate = (back * upper * sigma * (1.0 + gate * (1.0 - sigma))).astype(jnp.bfloat16)
    d_upper = (back * silu_gate).astype(jnp.bfloat16)
    grad_gate = jnp.dot(key_rows.T, d_gate, preferred_element_type=jnp.float32)
    grad_upper = jnp.dot(key_rows.T, d_upper, preferred_element_type=jnp.float32)
    grad_down = jnp.dot(hidden.T, outer, preferred_element_type=jnp.float32)
    return jnp.stack([grad_gate, grad_upper, grad_down])

def newton_schulz(matrix):
    wide = matrix.astype(jnp.float32)
    iterate = (wide / (jnp.sqrt(jnp.sum(wide * wide)) + 1e-07)).astype(jnp.bfloat16)
    for step in range(NS_STEPS):
        gram = jnp.dot(iterate, iterate.T, preferred_element_type=jnp.float32).astype(jnp.bfloat16)
        square = jnp.dot(gram, gram, preferred_element_type=jnp.float32)
        mixed = (-4.775 * gram.astype(jnp.float32) + 2.0315 * square).astype(jnp.bfloat16)
        iterate = (3.4445 * iterate.astype(jnp.float32) + jnp.dot(mixed, iterate, preferred_element_type=jnp.float32)).astype(jnp.bfloat16)
    return iterate

def renormed(weight, update):
    old = weight.astype(jnp.float32)
    fresh = old - update.astype(jnp.float32)
    scale = jnp.sqrt((lax.optimization_barrier(jnp.mean(old * old, axis=1, keepdims=True)) + 1e-06) / (lax.optimization_barrier(jnp.mean(fresh * fresh, axis=1, keepdims=True)) + 1e-06))
    return (fresh * scale).astype(jnp.bfloat16)

def apply_fast(query_rows, gate_w, up_w, down_w):
    gate = jnp.dot(query_rows, gate_w, preferred_element_type=jnp.float32)
    upper = jnp.dot(query_rows, up_w, preferred_element_type=jnp.float32)
    hidden = (jax.nn.silu(gate) * upper).astype(jnp.bfloat16)
    return jnp.dot(hidden, down_w, preferred_element_type=jnp.float32).astype(jnp.bfloat16)

def reference(keys, values, queries, rates, fast_weights):
    outputs = []
    weights_out = []
    for head in range(HEADS):
        cols = slice(head * DH, (head + 1) * DH)
        gate_w = fast_weights[head, 0]
        up_w = fast_weights[head, 1]
        down_w = fast_weights[head, 2]
        grads = swiglu_grads(keys[:, cols], values[:, cols], rates[head], gate_w, up_w, down_w)
        rounded = grads.astype(jnp.bfloat16)
        fresh = [renormed(fast_weights[head, which], newton_schulz(rounded[which])) for which in range(3)]
        weights_out.append(jnp.stack(fresh))
        outputs.append(apply_fast(queries[:, cols], fresh[0], fresh[1], fresh[2]))
    return (jnp.concatenate(outputs, axis=1), jnp.stack(weights_out))
```

```python
import functools

import jax
import jax.numpy as jnp
from jax import lax
from jax.experimental import pallas as pl
from jax.experimental.pallas import tpu as pltpu
from jax.sharding import PartitionSpec as P

NS_STEPS = 2
F32 = jnp.float32
BF16 = jnp.bfloat16
VMEM_SPEC = pl.BlockSpec(memory_space=pltpu.VMEM)
ANY_SPEC = pl.BlockSpec(memory_space=pl.ANY)
PARAMS = pltpu.CompilerParams(vmem_limit_bytes=40 * 1024 * 1024)


def place():
    me = lax.axis_index("tok")
    core = me % 2
    bit1 = (me // 2) % 2
    bit2 = (me // 4) % 2
    half = jnp.where(core == 0, bit1, bit2)
    quarter = jnp.where(core == 0, bit2, bit1)
    return core, half, quarter


def dot(a, b, ca=1, cb=0):
    return lax.dot_general(a, b, (((ca,), (cb,)), ((), ())), preferred_element_type=F32)


def pack_kernel(keys, values, rates, own, other):
    tokens, width = own.shape[1:]
    core, _, _ = place()
    for head, out in ((core, own), (1 - core, other)):
        cols = pl.ds(pl.multiple_of(head * width, width), width)
        out[0] = keys[:, cols]
        rate = jnp.where(head == 0, rates[0:1, :], rates[1:2, :])
        rate = jnp.broadcast_to(rate, (tokens, tokens)).T[:, 0:1]
        out[1] = (-rate * values[:, cols].astype(F32)).astype(BF16)


def grads_kernel(t0, t1, t2, t3, weights, send_a, send_b, keep_a, keep_b, keys, outer, gate_w, up_w, down_w, sems):
    tokens, width = t0.shape[1:]
    part = width // 2
    piece = part // 2
    core, half, quarter = place()
    cols = pl.ds(pl.multiple_of(half * part, part), part)
    copies = [
        pltpu.make_async_copy(weights.at[core, 0, :, cols], gate_w, sems.at[0]),
        pltpu.make_async_copy(weights.at[core, 1, :, cols], up_w, sems.at[1]),
        pltpu.make_async_copy(weights.at[core, 2, cols, :], down_w, sems.at[2]),
    ]
    for copy in copies:
        copy.start()
    for at, src in enumerate((t0, t1, t2, t3)):
        keys[at * tokens : (at + 1) * tokens, :] = src[0]
        outer[at * tokens : (at + 1) * tokens, :] = src[1]
    for copy in copies:
        copy.wait()
    k = keys[...]
    o = outer[...]
    for mine in (0, 1):
        at = (1 - quarter) if mine == 0 else quarter
        cut = pl.ds(pl.multiple_of(at * piece, piece), piece)
        gate = dot(k, gate_w[:, cut])
        upper = dot(k, up_w[:, cut])
        back = dot(o, down_w[cut, :], 1, 1)
        sigma = jax.nn.sigmoid(gate)
        silu_gate = gate * sigma
        hidden = (silu_gate * upper).astype(BF16)
        d_gate = (back * upper * sigma * (1.0 + gate * (1.0 - sigma))).astype(BF16)
        d_upper = (back * silu_gate).astype(BF16)
        out_a, out_b = (send_a, send_b) if mine == 0 else (keep_a, keep_b)
        out_a[0] = dot(k, d_gate, 0, 0).astype(out_a.dtype)
        out_a[1] = dot(k, d_upper, 0, 0).astype(out_a.dtype)
        out_b[...] = dot(hidden, o, 0, 0).astype(out_b.dtype)


def newton_schulz(matrix):
    wide = matrix.astype(F32)
    norm = jnp.sqrt(jnp.sum(wide * wide)) + 1e-07
    iterate = (wide / norm).astype(BF16)
    for _ in range(NS_STEPS):
        gram = dot(iterate, iterate, 1, 1).astype(BF16)
        mixed = (-4.775 * gram.astype(F32) + 2.0315 * dot(gram, gram)).astype(BF16)
        iterate = (3.4445 * iterate.astype(F32) + dot(mixed, iterate)).astype(BF16)
    return iterate


def renormed(old, update):
    old = old.astype(F32)
    fresh = old - update.astype(F32)
    scale = jnp.sqrt(
        (jnp.mean(old * old, axis=1, keepdims=True) + 1e-06)
        / (jnp.mean(fresh * fresh, axis=1, keepdims=True) + 1e-06)
    )
    return (fresh * scale).astype(BF16)


def ns_kernel(first, rows_cut, p_own, p_second, p_first, p_both, weights, new, total, old, sem):
    count = new.shape[0]
    core, half, quarter = place()
    copy = pltpu.make_async_copy(weights.at[core, pl.ds(first, count)], old, sem)
    copy.start()
    for piece, h, q in (
        (p_own, half, quarter),
        (p_second, half, 1 - quarter),
        (p_first, 1 - half, quarter),
        (p_both, 1 - half, 1 - quarter),
    ):
        size = piece.shape[0] if rows_cut else piece.shape[2]
        cut = pl.ds(pl.multiple_of((2 * h + q) * size, size), size)
        if rows_cut:
            total[0, cut, :] = piece[...]
        else:
            for at in range(count):
                total[at, :, cut] = piece[at]
    updates = [newton_schulz(total[at]) for at in range(count)]
    copy.wait()
    for at in range(count):
        new[at] = renormed(old[at], updates[at])


def updated(first, rows_cut, pieces, weights):
    width = weights.shape[3]
    count = 1 if rows_cut else pieces[0].shape[0]
    return pl.pallas_call(
        functools.partial(ns_kernel, first, rows_cut),
        out_shape=jax.ShapeDtypeStruct((count, width, width), BF16),
        in_specs=[VMEM_SPEC] * 4 + [ANY_SPEC],
        out_specs=VMEM_SPEC,
        scratch_shapes=[
            pltpu.VMEM((count, width, width), BF16),
            pltpu.VMEM((count, width, width), BF16),
            pltpu.SemaphoreType.DMA,
        ],
        compiler_params=PARAMS,
    )(*pieces, weights)


def gate_up_kernel(queries, own, other, hidden, new_weights, sems):
    width = own.shape[2]
    core, _, _ = place()
    copies = []
    for at, (head, part) in enumerate(((core, own), (1 - core, other))):
        copy = pltpu.make_async_copy(part, new_weights.at[head, pl.ds(0, 2)], sems.at[at])
        copy.start()
        copies.append(copy)
    for head, part in ((core, own), (1 - core, other)):
        cols = pl.ds(pl.multiple_of(head * width, width), width)
        gate = dot(queries[:, cols], part[0])
        upper = dot(queries[:, cols], part[1])
        hidden[:, cols] = (gate * jax.nn.sigmoid(gate) * upper).astype(BF16)
    for copy in copies:
        copy.wait()


def down_kernel(hidden, own, other, held, readout, new_weights, sems):
    width = own.shape[2]
    core, _, _ = place()
    copies = []
    for at, (head, part) in enumerate(((core, own), (1 - core, other))):
        copy = pltpu.make_async_copy(part, new_weights.at[head, pl.ds(2, 1)], sems.at[at])
        copy.start()
        copies.append(copy)
    for head, part in ((core, own), (1 - core, other)):
        cols = pl.ds(pl.multiple_of(head * width, width), width)
        readout[:, cols] = dot(hidden[:, cols], part[0]).astype(BF16)
    for copy in copies:
        copy.wait()


def body(size, keys, values, queries, rates, fast_weights):
    tokens = keys.shape[0]
    heads, _, width, _ = fast_weights.shape
    quarter = width // 4
    sibling = [(i, i ^ 1) for i in range(size)]
    first = [(i, i ^ (2 if i % 2 == 0 else 4)) for i in range(size)]
    second = [(i, i ^ (4 if i % 2 == 0 else 2)) for i in range(size)]
    across = [(i, i ^ 1 ^ (4 if i % 2 == 0 else 2)) for i in range(size)]
    rest = [[(i, i ^ (1 << bit)) for i in range(size)] for bit in range(3, size.bit_length() - 1)]

    def move(value, pairs):
        return lax.ppermute(value, "tok", pairs)

    pair = jax.ShapeDtypeStruct((2, tokens, width), BF16)
    own, other = pl.pallas_call(
        pack_kernel,
        out_shape=(pair, pair),
        in_specs=[VMEM_SPEC] * 3,
        out_specs=(VMEM_SPEC, VMEM_SPEC),
        compiler_params=PARAMS,
    )(keys, values, rates)
    blocks = (own, move(other, sibling), move(own, first), move(other, across))
    shape_a, shape_b = (2, width, quarter), (quarter, width)
    send_a, send_b, keep_a, keep_b = pl.pallas_call(
        grads_kernel,
        out_shape=(
            jax.ShapeDtypeStruct(shape_a, BF16),
            jax.ShapeDtypeStruct(shape_b, BF16),
            jax.ShapeDtypeStruct(shape_a, F32),
            jax.ShapeDtypeStruct(shape_b, F32),
        ),
        in_specs=[VMEM_SPEC] * 4 + [ANY_SPEC],
        out_specs=(VMEM_SPEC,) * 4,
        scratch_shapes=[
            pltpu.VMEM((4 * tokens, width), BF16),
            pltpu.VMEM((4 * tokens, width), BF16),
            pltpu.VMEM((width, width // 2), BF16),
            pltpu.VMEM((width, width // 2), BF16),
            pltpu.VMEM((width // 2, width), BF16),
            pltpu.SemaphoreType.DMA((3,)),
        ],
        compiler_params=PARAMS,
    )(*blocks, fast_weights)

    def reduced(send, keep):
        part = (keep + move(send, second).astype(F32)).astype(BF16)
        for pairs in rest:
            part = (part.astype(F32) + move(part, pairs).astype(F32)).astype(BF16)
        return part

    def gathered(part):
        over_second = move(part, second)
        over_first = move(part, first)
        return part, over_second, over_first, move(over_second, first)

    sum_a = reduced(send_a, keep_a)
    sum_b = reduced(send_b, keep_b)
    new_a = updated(0, False, gathered(sum_a), fast_weights)
    swap_a = move(new_a, sibling)
    hidden, new_weights = pl.pallas_call(
        gate_up_kernel,
        out_shape=(
            jax.ShapeDtypeStruct(queries.shape, BF16),
            jax.ShapeDtypeStruct(fast_weights.shape, BF16),
        ),
        in_specs=[VMEM_SPEC] * 3,
        out_specs=(VMEM_SPEC, ANY_SPEC),
        scratch_shapes=[pltpu.SemaphoreType.DMA((2,))],
        compiler_params=PARAMS,
    )(queries, new_a, swap_a)
    new_b = updated(2, True, gathered(sum_b), fast_weights)
    swap_b = move(new_b, sibling)
    return pl.pallas_call(
        down_kernel,
        out_shape=(
            jax.ShapeDtypeStruct(queries.shape, BF16),
            jax.ShapeDtypeStruct(fast_weights.shape, BF16),
        ),
        in_specs=[VMEM_SPEC] * 3 + [ANY_SPEC],
        out_specs=(VMEM_SPEC, ANY_SPEC),
        scratch_shapes=[pltpu.SemaphoreType.DMA((2,))],
        input_output_aliases={3: 1},
        compiler_params=PARAMS,
    )(hidden, new_b, swap_b, new_weights)


def solution(mesh):
    return jax.shard_map(
        functools.partial(body, mesh.shape["tok"]),
        mesh=mesh,
        in_specs=(
            P(("grp", "tok"), None),
            P(("grp", "tok"), None),
            P(("grp", "tok"), None),
            P(None, ("grp", "tok")),
            P(),
        ),
        out_specs=(P(("grp", "tok"), None), P("grp", None, None, None)),
        check_vma=False,
    )
```

```python
import functools

import jax
import jax.numpy as jnp
from jax import lax
from jax.experimental import pallas as pl
from jax.experimental.pallas import tpu as pltpu
from jax.sharding import PartitionSpec as P

NS_STEPS = 2
F32 = jnp.float32
BF16 = jnp.bfloat16
VMEM_SPEC = pl.BlockSpec(memory_space=pltpu.VMEM)
ANY_SPEC = pl.BlockSpec(memory_space=pl.ANY)
PARAMS = pltpu.CompilerParams(vmem_limit_bytes=40 * 1024 * 1024)
WHOLE_VMEM = pltpu.CompilerParams(vmem_limit_bytes=62 * 1024 * 1024)


def place():
    me = lax.axis_index("tok")
    core = me % 2
    bit1 = (me // 2) % 2
    bit2 = (me // 4) % 2
    half = jnp.where(core == 0, bit1, bit2)
    quarter = jnp.where(core == 0, bit2, bit1)
    return core, half, quarter


def dot(a, b, ca=1, cb=0):
    return lax.dot_general(a, b, (((ca,), (cb,)), ((), ())), preferred_element_type=F32)


def span(at, size):
    return pl.ds(pl.multiple_of(at * size, size), size)


def pack_kernel(keys, values, rates, own, other, held, rate, sems):
    tokens, width = own.shape[1:]
    core, _, _ = place()
    copies = [
        pltpu.make_async_copy(values, held, sems.at[0]),
        pltpu.make_async_copy(rates, rate, sems.at[1]),
    ]
    for at, (head, out) in enumerate(((core, own), (1 - core, other))):
        copies.append(pltpu.make_async_copy(keys.at[:, span(head, width)], out.at[0], sems.at[2 + at]))
    for copy in copies:
        copy.start()
    for copy in copies:
        copy.wait()
    for head, out in ((core, own), (1 - core, other)):
        row = jnp.where(head == 0, rate[0:1, :], rate[1:2, :])
        column = jnp.broadcast_to(row, (tokens, tokens)).T[:, 0:1]
        out[1] = (-column * held[:, span(head, width)].astype(F32)).astype(BF16)


def token_grads(k, o, weights, cut):
    gate = dot(k, weights[0, :, cut])
    upper = dot(k, weights[1, :, cut])
    back = dot(o, weights[2, cut, :], 1, 1)
    sigma = jax.nn.sigmoid(gate)
    silu_gate = gate * sigma
    hidden = (silu_gate * upper).astype(BF16)
    d_gate = (back * upper * sigma * (1.0 + gate * (1.0 - sigma))).astype(BF16)
    d_upper = (back * silu_gate).astype(BF16)
    return dot(k, d_gate, 0, 0), dot(k, d_upper, 0, 0), dot(hidden, o, 0, 0)


def cuts(width):
    _, half, quarter = place()
    return span(2 * half + 1 - quarter, width // 4), span(2 * half + quarter, width // 4)


def near_kernel(t0, t1, weights, send, keep, mine, keys, outer, sem):
    tokens, width = t0.shape[1:]
    piece = width // 4
    core, _, _ = place()
    copy = pltpu.make_async_copy(weights.at[core], mine, sem)
    copy.start()
    for at, src in enumerate((t0, t1)):
        keys[at * tokens : (at + 1) * tokens, :] = src[0]
        outer[at * tokens : (at + 1) * tokens, :] = src[1]
    copy.wait()
    for out, cut in zip((send, keep), cuts(width)):
        gate, upper, down = token_grads(keys[...], outer[...], mine, cut)
        out[0] = gate
        out[1] = upper
        for at in range(width // piece):
            out[2, at * piece : (at + 1) * piece, :] = down[:, at * piece : (at + 1) * piece]


def far_kernel(t2, t3, mine, near_send, near_keep, *refs):
    outs, (keys, outer) = refs[:6], refs[6:]
    tokens, width = t2.shape[1:]
    piece = width // 4
    for at, src in enumerate((t2, t3)):
        keys[at * tokens : (at + 1) * tokens, :] = src[0]
        outer[at * tokens : (at + 1) * tokens, :] = src[1]
    for out, near, cut in zip((outs[:3], outs[3:]), (near_send, near_keep), cuts(width)):
        gate, upper, down = token_grads(keys[...], outer[...], mine, cut)
        out[0][...] = (near[0] + gate).astype(out[0].dtype)
        out[1][...] = (near[1] + upper).astype(out[1].dtype)
        for at in range(width // piece):
            rows = slice(at * piece, (at + 1) * piece)
            out[2][rows, :] = (near[2, rows, :] + down[:, rows]).astype(out[2].dtype)


def newton_schulz(matrix):
    wide = matrix.astype(F32)
    norm = jnp.sqrt(jnp.sum(wide * wide)) + 1e-07
    iterate = (wide / norm).astype(BF16)
    for _ in range(NS_STEPS):
        gram = dot(iterate, iterate, 1, 1).astype(BF16)
        mixed = (-4.775 * gram.astype(F32) + 2.0315 * dot(gram, gram)).astype(BF16)
        iterate = (3.4445 * iterate.astype(F32) + dot(mixed, iterate)).astype(BF16)
    return iterate


def renormed(old, update):
    old = old.astype(F32)
    fresh = old - update.astype(F32)
    scale = jnp.sqrt(
        (jnp.mean(old * old, axis=1, keepdims=True) + 1e-06)
        / (jnp.mean(fresh * fresh, axis=1, keepdims=True) + 1e-06)
    )
    return (fresh * scale).astype(BF16)


def ns_kernel(which, earlier, mine, *refs):
    count = len(which)
    pieces, (total, sems) = refs[: 4 * count], refs[-2:]
    if earlier:
        before, new, new_weights = refs[4 * count : -2]
    else:
        new = refs[4 * count]
    _, width, _ = new.shape
    size = width // 4
    core, half, quarter = place()
    places = ((half, quarter), (half, 1 - quarter), (1 - half, quarter), (1 - half, 1 - quarter))
    for at, matrix in enumerate(which):
        for (h, q), piece in zip(places, pieces[4 * at : 4 * at + 4]):
            cut = span(2 * h + q, size)
            if matrix < 2:
                total[at, :, cut] = piece[...]
            else:
                for block in range(width // size):
                    rows = slice(block * size, (block + 1) * size)
                    total[at, cut, rows] = piece[rows, :]
    copies = []
    if earlier:
        for at, matrix in enumerate(earlier):
            copy = pltpu.make_async_copy(before.at[at], new_weights.at[core, matrix], sems.at[at])
            copy.start()
            copies.append(copy)
    updates = [newton_schulz(total[at]) for at in range(count)]
    for at, matrix in enumerate(which):
        new[at] = renormed(mine[matrix], updates[at])
    for copy in copies:
        copy.wait()


def updated(which, pieces, mine, earlier=(), before=None):
    heads, width = 2, mine.shape[2]
    count = len(which)
    flat = [piece for four in pieces for piece in four]
    out = [jax.ShapeDtypeStruct((count, width, width), BF16)]
    if earlier:
        flat.append(before)
        out.append(jax.ShapeDtypeStruct((heads, *mine.shape), BF16))
    return pl.pallas_call(
        functools.partial(ns_kernel, which, earlier),
        out_shape=out,
        in_specs=[VMEM_SPEC] * (len(flat) + 1),
        out_specs=[VMEM_SPEC, ANY_SPEC][: len(out)],
        scratch_shapes=[
            pltpu.VMEM((count, width, width), BF16),
            pltpu.SemaphoreType.DMA((max(1, len(earlier)),)),
        ],
        compiler_params=PARAMS,
    )(mine, *flat)


def gate_up_kernel(queries, own, other, own_down, held, hidden, new_weights, sems):
    width = own.shape[2]
    core, _, _ = place()
    copies = [
        pltpu.make_async_copy(other, new_weights.at[1 - core, pl.ds(0, 2)], sems.at[0]),
        pltpu.make_async_copy(own_down, new_weights.at[core, pl.ds(2, 1)], sems.at[1]),
    ]
    for copy in copies:
        copy.start()
    for head, part in ((core, own), (1 - core, other)):
        cols = span(head, width)
        gate = dot(queries[:, cols], part[0])
        upper = dot(queries[:, cols], part[1])
        hidden[:, cols] = (gate * jax.nn.sigmoid(gate) * upper).astype(BF16)
    for copy in copies:
        copy.wait()


def down_kernel(hidden, own, other, held, readout, new_weights, sems):
    width = own.shape[2]
    core, _, _ = place()
    copy = pltpu.make_async_copy(other, new_weights.at[1 - core, pl.ds(2, 1)], sems.at[0])
    copy.start()
    for head, part in ((core, own), (1 - core, other)):
        cols = span(head, width)
        readout[:, cols] = dot(hidden[:, cols], part[0]).astype(BF16)
    copy.wait()


def body(size, keys, values, queries, rates, fast_weights):
    tokens = keys.shape[0]
    heads, _, width, _ = fast_weights.shape
    quarter = width // 4
    sibling = [(i, i ^ 1) for i in range(size)]
    first = [(i, i ^ (2 if i % 2 == 0 else 4)) for i in range(size)]
    second = [(i, i ^ (4 if i % 2 == 0 else 2)) for i in range(size)]
    across = [(i, i ^ 1 ^ (4 if i % 2 == 0 else 2)) for i in range(size)]
    rest = [[(i, i ^ (1 << bit)) for i in range(size)] for bit in range(3, size.bit_length() - 1)]

    def move(value, pairs):
        return lax.ppermute(value, "tok", pairs)

    def tie(*values):
        return lax.optimization_barrier(values)

    pair = jax.ShapeDtypeStruct((2, tokens, width), BF16)
    own, other = pl.pallas_call(
        pack_kernel,
        out_shape=(pair, pair),
        in_specs=[ANY_SPEC] * 3,
        out_specs=(VMEM_SPEC, VMEM_SPEC),
        scratch_shapes=[
            pltpu.VMEM(values.shape, BF16),
            pltpu.VMEM(rates.shape, F32),
            pltpu.SemaphoreType.DMA((4,)),
        ],
        compiler_params=WHOLE_VMEM,
    )(keys, values, rates)
    part16 = jax.ShapeDtypeStruct((width, quarter), BF16)
    part32 = jax.ShapeDtypeStruct((width, quarter), F32)
    three32 = jax.ShapeDtypeStruct((3, width, quarter), F32)
    rows_scratch = [pltpu.VMEM((2 * tokens, width), BF16)] * 2
    near_send, near_keep, mine = pl.pallas_call(
        near_kernel,
        out_shape=(three32, three32, jax.ShapeDtypeStruct((3, width, width), BF16)),
        in_specs=[VMEM_SPEC] * 2 + [ANY_SPEC],
        out_specs=(VMEM_SPEC,) * 3,
        scratch_shapes=rows_scratch + [pltpu.SemaphoreType.DMA],
        compiler_params=PARAMS,
    )(own, move(other, sibling), fast_weights)
    outs = pl.pallas_call(
        far_kernel,
        out_shape=(part16,) * 3 + (part32,) * 3,
        in_specs=[VMEM_SPEC] * 5,
        out_specs=(VMEM_SPEC,) * 6,
        scratch_shapes=rows_scratch,
        compiler_params=PARAMS,
    )(move(own, first), move(other, across), mine, near_send, near_keep)
    send, keep = outs[:3], outs[3:]

    def reduced(at):
        return (keep[at] + move(send[at], second).astype(F32)).astype(BF16)

    def crossed(part):
        for pairs in rest:
            part = (part.astype(F32) + move(part, pairs).astype(F32)).astype(BF16)
        return part

    def pieces(part):
        over = move(part, second)
        return part, over, move(part, first), move(over, first)

    four = [pieces(crossed(reduced(at))) for at in range(3)]
    flat = tie(*four[0], *four[1], *four[2])
    (new_a,) = updated((0, 1), (flat[0:4], flat[4:8]), mine)
    new_d, new_weights = updated((2,), (flat[8:12],), mine, (0, 1), new_a)
    hidden, new_weights = pl.pallas_call(
        gate_up_kernel,
        out_shape=(
            jax.ShapeDtypeStruct(queries.shape, BF16),
            jax.ShapeDtypeStruct(fast_weights.shape, BF16),
        ),
        in_specs=[VMEM_SPEC] * 4 + [ANY_SPEC],
        out_specs=(VMEM_SPEC, ANY_SPEC),
        scratch_shapes=[pltpu.SemaphoreType.DMA((2,))],
        input_output_aliases={4: 1},
        compiler_params=PARAMS,
    )(queries, new_a, move(new_a, sibling), new_d, new_weights)


    return pl.pallas_call(
        down_kernel,
        out_shape=(
            jax.ShapeDtypeStruct(queries.shape, BF16),
            jax.ShapeDtypeStruct(fast_weights.shape, BF16),
        ),
        in_specs=[VMEM_SPEC] * 3 + [ANY_SPEC],
        out_specs=(VMEM_SPEC, ANY_SPEC),
        scratch_shapes=[pltpu.SemaphoreType.DMA((1,))],
        input_output_aliases={3: 1},
        compiler_params=PARAMS,
    )(hidden, new_d, move(new_d, sibling), new_weights)


def solution(mesh):
    return jax.shard_map(
        functools.partial(body, mesh.shape["tok"]),
        mesh=mesh,
        in_specs=(
            P(("grp", "tok"), None),
            P(("grp", "tok"), None),
            P(("grp", "tok"), None),
            P(None, ("grp", "tok")),
            P(),
        ),
        out_specs=(P(("grp", "tok"), None), P("grp", None, None, None)),
        check_vma=False,
    )
```

```python
import functools

import jax
import jax.numpy as jnp
from jax import lax
from jax.experimental import pallas as pl
from jax.experimental.pallas import tpu as pltpu
from jax.sharding import PartitionSpec as P

NS_STEPS = 2
F32 = jnp.float32
BF16 = jnp.bfloat16
VMEM_SPEC = pl.BlockSpec(memory_space=pltpu.VMEM)
ANY_SPEC = pl.BlockSpec(memory_space=pl.ANY)
PARAMS = pltpu.CompilerParams(vmem_limit_bytes=40 * 1024 * 1024)
WHOLE_VMEM = pltpu.CompilerParams(vmem_limit_bytes=62 * 1024 * 1024)


def place():
    me = lax.axis_index("tok")
    core = me % 2
    bit1 = (me // 2) % 2
    bit2 = (me // 4) % 2
    half = jnp.where(core == 0, bit1, bit2)
    quarter = jnp.where(core == 0, bit2, bit1)
    return core, half, quarter


def dot(a, b, ca=1, cb=0):
    return lax.dot_general(a, b, (((ca,), (cb,)), ((), ())), preferred_element_type=F32)


def span(at, size):
    return pl.ds(pl.multiple_of(at * size, size), size)


def pack_kernel(keys, values, rates, own, other, held, rate, sems):
    tokens, width = own.shape[1:]
    core, _, _ = place()
    copies = [
        pltpu.make_async_copy(values, held, sems.at[0]),
        pltpu.make_async_copy(rates, rate, sems.at[1]),
    ]
    for at, (head, out) in enumerate(((core, own), (1 - core, other))):
        copies.append(pltpu.make_async_copy(keys.at[:, span(head, width)], out.at[0], sems.at[2 + at]))
    for copy in copies:
        copy.start()
    for copy in copies:
        copy.wait()
    for head, out in ((core, own), (1 - core, other)):
        row = jnp.where(head == 0, rate[0:1, :], rate[1:2, :])
        column = jnp.broadcast_to(row, (tokens, tokens)).T[:, 0:1]
        out[1] = (-column * held[:, span(head, width)].astype(F32)).astype(BF16)


def token_grads(k, o, weights, cut):
    gate = dot(k, weights[0, :, cut])
    upper = dot(k, weights[1, :, cut])
    back = dot(o, weights[2, cut, :], 1, 1)
    sigma = jax.nn.sigmoid(gate)
    silu_gate = gate * sigma
    hidden = (silu_gate * upper).astype(BF16)
    d_gate = (back * upper * sigma * (1.0 + gate * (1.0 - sigma))).astype(BF16)
    d_upper = (back * silu_gate).astype(BF16)
    return dot(k, d_gate, 0, 0), dot(k, d_upper, 0, 0), dot(hidden, o, 0, 0)


def cuts(width):
    _, half, quarter = place()
    return span(2 * half + 1 - quarter, width // 4), span(2 * half + quarter, width // 4)


def near_kernel(t0, t1, weights, send, keep, mine, keys, outer, sem):
    tokens, width = t0.shape[1:]
    piece = width // 4
    core, _, _ = place()
    copy = pltpu.make_async_copy(weights.at[core], mine, sem)
    copy.start()
    for at, src in enumerate((t0, t1)):
        keys[at * tokens : (at + 1) * tokens, :] = src[0]
        outer[at * tokens : (at + 1) * tokens, :] = src[1]
    copy.wait()
    for out, cut in zip((send, keep), cuts(width)):
        gate, upper, down = token_grads(keys[...], outer[...], mine, cut)
        out[0] = gate
        out[1] = upper
        for at in range(width // piece):
            out[2, at * piece : (at + 1) * piece, :] = down[:, at * piece : (at + 1) * piece]


def far_kernel(t2, t3, mine, near_send, near_keep, *refs):
    outs, (keys, outer) = refs[:6], refs[6:]
    tokens, width = t2.shape[1:]
    piece = width // 4
    for at, src in enumerate((t2, t3)):
        keys[at * tokens : (at + 1) * tokens, :] = src[0]
        outer[at * tokens : (at + 1) * tokens, :] = src[1]
    for out, near, cut in zip((outs[:3], outs[3:]), (near_send, near_keep), cuts(width)):
        gate, upper, down = token_grads(keys[...], outer[...], mine, cut)
        out[0][...] = (near[0] + gate).astype(out[0].dtype)
        out[1][...] = (near[1] + upper).astype(out[1].dtype)
        for at in range(width // piece):
            rows = slice(at * piece, (at + 1) * piece)
            out[2][rows, :] = (near[2, rows, :] + down[:, rows]).astype(out[2].dtype)


def newton_schulz(matrix):
    wide = matrix.astype(F32)
    norm = jnp.sqrt(jnp.sum(wide * wide)) + 1e-07
    iterate = (wide * (1.0 / norm)).astype(BF16)
    half = matrix.shape[0] // 2
    for _ in range(NS_STEPS):
        upper = dot(iterate[:half], iterate, 1, 1).astype(BF16)
        corner = dot(iterate[half:], iterate[half:], 1, 1).astype(BF16)
        lower = jnp.concatenate([upper[:, half:].T, corner], axis=1)
        gram = jnp.concatenate([upper, lower], axis=0)
        mixed = (-4.775 * gram.astype(F32) + 2.0315 * dot(gram, gram)).astype(BF16)
        iterate = (3.4445 * iterate.astype(F32) + dot(mixed, iterate)).astype(BF16)
    return iterate


def renormed(old, update):
    old = old.astype(F32)
    fresh = old - update.astype(F32)
    scale = jnp.sqrt(
        (jnp.mean(old * old, axis=1, keepdims=True) + 1e-06)
        / (jnp.mean(fresh * fresh, axis=1, keepdims=True) + 1e-06)
    )
    return (fresh * scale).astype(BF16)


def ns_kernel(which, earlier, mine, *refs):
    count = len(which)
    pieces, (total, sems) = refs[: 4 * count], refs[-2:]
    if earlier:
        before, new, new_weights = refs[4 * count], *refs[-4:-2]
    else:
        new = refs[4 * count]
    _, width, _ = new.shape
    size = width // 4
    core, half, quarter = place()
    places = ((half, quarter), (half, 1 - quarter), (1 - half, quarter), (1 - half, 1 - quarter))
    for at, matrix in enumerate(which):
        for (h, q), piece in zip(places, pieces[4 * at : 4 * at + 4]):
            cut = span(2 * h + q, size)
            if matrix < 2:
                total[at, :, cut] = piece[...]
            else:
                for block in range(width // size):
                    rows = slice(block * size, (block + 1) * size)
                    total[at, cut, rows] = piece[rows, :]
    copies = []
    if earlier:
        for at, matrix in enumerate(earlier):
            copy = pltpu.make_async_copy(before.at[at], new_weights.at[core, matrix], sems.at[at])
            copy.start()
            copies.append(copy)
    updates = [newton_schulz(total[at]) for at in range(count)]
    for at, matrix in enumerate(which):
        new[at] = renormed(mine[matrix], updates[at])
    for copy in copies:
        copy.wait()


def updated(which, pieces, mine, earlier=(), before=None, held=None):
    heads, width = 2, mine.shape[2]
    count = len(which)
    flat = [piece for four in pieces for piece in four]
    out = [jax.ShapeDtypeStruct((count, width, width), BF16)]
    if earlier:
        flat.append(before)
        out.append(jax.ShapeDtypeStruct((heads, *mine.shape), BF16))
    specs = [VMEM_SPEC] * (len(flat) + 1)
    if held is not None:
        flat.append(held)
        specs.append(ANY_SPEC)
    return pl.pallas_call(
        functools.partial(ns_kernel, which, earlier),
        out_shape=out,
        in_specs=specs,
        input_output_aliases={} if held is None else {len(flat): 1},
        out_specs=[VMEM_SPEC, ANY_SPEC][: len(out)],
        scratch_shapes=[
            pltpu.VMEM((count, width, width), BF16),
            pltpu.SemaphoreType.DMA((max(1, len(earlier)),)),
        ],
        compiler_params=PARAMS,
        cost_estimate=pl.CostEstimate(
            flops=120 * NS_STEPS * count * width**3, bytes_accessed=64 * count * width**2, transcendentals=0
        ),
    )(mine, *flat)


def gate_up_kernel(queries, own, other, own_down, held, hidden, new_weights, sems):
    width = own.shape[2]
    core, _, _ = place()
    copies = [
        pltpu.make_async_copy(other, new_weights.at[1 - core, pl.ds(0, 2)], sems.at[0]),
        pltpu.make_async_copy(own_down, new_weights.at[core, pl.ds(2, 1)], sems.at[1]),
    ]
    for copy in copies:
        copy.start()
    for head, part in ((core, own), (1 - core, other)):
        cols = span(head, width)
        gate = dot(queries[:, cols], part[0])
        upper = dot(queries[:, cols], part[1])
        hidden[:, cols] = (gate * jax.nn.sigmoid(gate) * upper).astype(BF16)
    for copy in copies:
        copy.wait()


def down_kernel(hidden, own, other, held, readout, new_weights, sems):
    width = own.shape[2]
    core, _, _ = place()
    copy = pltpu.make_async_copy(other, new_weights.at[1 - core, pl.ds(2, 1)], sems.at[0])
    copy.start()
    for head, part in ((core, own), (1 - core, other)):
        cols = span(head, width)
        readout[:, cols] = dot(hidden[:, cols], part[0]).astype(BF16)
    copy.wait()


def body(size, keys, values, queries, rates, fast_weights):
    tokens = keys.shape[0]
    heads, _, width, _ = fast_weights.shape
    quarter = width // 4
    sibling = [(i, i ^ 1) for i in range(size)]
    first = [(i, i ^ (2 if i % 2 == 0 else 4)) for i in range(size)]
    second = [(i, i ^ (4 if i % 2 == 0 else 2)) for i in range(size)]
    across = [(i, i ^ 1 ^ (4 if i % 2 == 0 else 2)) for i in range(size)]
    rest = [[(i, i ^ (1 << bit)) for i in range(size)] for bit in range(3, size.bit_length() - 1)]

    def move(value, pairs):
        return lax.ppermute(value, "tok", pairs)

    def tie(*values):
        return lax.optimization_barrier(values)

    pair = jax.ShapeDtypeStruct((2, tokens, width), BF16)
    own, other = pl.pallas_call(
        pack_kernel,
        out_shape=(pair, pair),
        in_specs=[ANY_SPEC] * 3,
        out_specs=(VMEM_SPEC, VMEM_SPEC),
        scratch_shapes=[
            pltpu.VMEM(values.shape, BF16),
            pltpu.VMEM(rates.shape, F32),
            pltpu.SemaphoreType.DMA((4,)),
        ],
        compiler_params=WHOLE_VMEM,
    )(keys, values, rates)
    part16 = jax.ShapeDtypeStruct((width, quarter), BF16)
    part32 = jax.ShapeDtypeStruct((width, quarter), F32)
    three32 = jax.ShapeDtypeStruct((3, width, quarter), F32)
    rows_scratch = [pltpu.VMEM((2 * tokens, width), BF16)] * 2
    near_send, near_keep, mine = pl.pallas_call(
        near_kernel,
        out_shape=(three32, three32, jax.ShapeDtypeStruct((3, width, width), BF16)),
        in_specs=[VMEM_SPEC] * 2 + [ANY_SPEC],
        out_specs=(VMEM_SPEC,) * 3,
        scratch_shapes=rows_scratch + [pltpu.SemaphoreType.DMA],
        compiler_params=PARAMS,
    )(own, move(other, sibling), fast_weights)
    outs = pl.pallas_call(
        far_kernel,
        out_shape=(part16,) * 3 + (part32,) * 3,
        in_specs=[VMEM_SPEC] * 5,
        out_specs=(VMEM_SPEC,) * 6,
        scratch_shapes=rows_scratch,
        compiler_params=PARAMS,
    )(move(own, first), move(other, across), mine, near_send, near_keep)
    send, keep = outs[:3], outs[3:]

    def reduced(at):
        return (keep[at] + move(send[at], second).astype(F32)).astype(BF16)

    def crossed(part):
        for pairs in rest:
            part = (part.astype(F32) + move(part, pairs).astype(F32)).astype(BF16)
        return part

    def pieces(part):
        over = move(part, second)
        return part, over, move(part, first), move(over, first)

    parts = [reduced(at) for at in range(3)]
    sums = [crossed(parts[0]), crossed(parts[1])]
    sums[0], part_d = tie(sums[0], parts[2])
    four = [pieces(s) for s in (*sums, crossed(part_d))]
    (new_a,) = updated((0, 1), four[:2], mine)
    new_d, new_weights = updated((2,), four[2:], mine, (0, 1), new_a)
    hidden, new_weights = pl.pallas_call(
        gate_up_kernel,
        out_shape=(
            jax.ShapeDtypeStruct(queries.shape, BF16),
            jax.ShapeDtypeStruct(fast_weights.shape, BF16),
        ),
        in_specs=[VMEM_SPEC] * 4 + [ANY_SPEC],
        out_specs=(VMEM_SPEC, ANY_SPEC),
        scratch_shapes=[pltpu.SemaphoreType.DMA((2,))],
        input_output_aliases={4: 1},
        compiler_params=PARAMS,
    )(queries, new_a, move(new_a, sibling), new_d, new_weights)


    return pl.pallas_call(
        down_kernel,
        out_shape=(
            jax.ShapeDtypeStruct(queries.shape, BF16),
            jax.ShapeDtypeStruct(fast_weights.shape, BF16),
        ),
        in_specs=[VMEM_SPEC] * 3 + [ANY_SPEC],
        out_specs=(VMEM_SPEC, ANY_SPEC),
        scratch_shapes=[pltpu.SemaphoreType.DMA((1,))],
        input_output_aliases={3: 1},
        compiler_params=PARAMS,
    )(hidden, new_d, move(new_d, sibling), new_weights)


def solution(mesh):
    return jax.shard_map(
        functools.partial(body, mesh.shape["tok"]),
        mesh=mesh,
        in_specs=(
            P(("grp", "tok"), None),
            P(("grp", "tok"), None),
            P(("grp", "tok"), None),
            P(None, ("grp", "tok")),
            P(),
        ),
        out_specs=(P(("grp", "tok"), None), P("grp", None, None, None)),
        check_vma=False,
    )
```

```python
import functools

import jax
import jax.numpy as jnp
from jax import lax
from jax.experimental import pallas as pl
from jax.experimental.pallas import tpu as pltpu
from jax.sharding import PartitionSpec as P

NS_STEPS = 2
F32 = jnp.float32
BF16 = jnp.bfloat16
VMEM_SPEC = pl.BlockSpec(memory_space=pltpu.VMEM)
ANY_SPEC = pl.BlockSpec(memory_space=pl.ANY)
PARAMS = pltpu.CompilerParams(vmem_limit_bytes=40 * 1024 * 1024)
WHOLE_VMEM = pltpu.CompilerParams(vmem_limit_bytes=62 * 1024 * 1024)


def place():
    me = lax.axis_index("tok")
    core = me % 2
    bit1 = (me // 2) % 2
    bit2 = (me // 4) % 2
    half = jnp.where(core == 0, bit1, bit2)
    quarter = jnp.where(core == 0, bit2, bit1)
    return core, half, quarter


def dot(a, b, ca=1, cb=0):
    return lax.dot_general(a, b, (((ca,), (cb,)), ((), ())), preferred_element_type=F32)


def span(at, size):
    return pl.ds(pl.multiple_of(at * size, size), size)


def pack_kernel(keys, values, rates, own, other, held, rate, sems):
    tokens, width = own.shape[1:]
    core, _, _ = place()
    copies = [
        pltpu.make_async_copy(values, held, sems.at[0]),
        pltpu.make_async_copy(rates, rate, sems.at[1]),
    ]
    for at, (head, out) in enumerate(((core, own), (1 - core, other))):
        copies.append(pltpu.make_async_copy(keys.at[:, span(head, width)], out.at[0], sems.at[2 + at]))
    for copy in copies:
        copy.start()
    for copy in copies[:2]:
        copy.wait()
    for head, out in ((core, own), (1 - core, other)):
        row = jnp.where(head == 0, rate[0:1, :], rate[1:2, :])
        column = jnp.broadcast_to(row, (tokens, tokens)).T[:, 0:1]
        out[1] = (-column * held[:, span(head, width)].astype(F32)).astype(BF16)
    for copy in copies[2:]:
        copy.wait()


def token_parts(k, o, weights, cut):
    gate = dot(k, weights[0, :, cut])
    upper = dot(k, weights[1, :, cut])
    back = dot(o, weights[2, cut, :], 1, 1)
    sigma = jax.nn.sigmoid(gate)
    silu_gate = gate * sigma
    hidden = (silu_gate * upper).astype(BF16)
    d_gate = (back * upper * sigma * (1.0 + gate * (1.0 - sigma))).astype(BF16)
    d_upper = (back * silu_gate).astype(BF16)
    return hidden, d_gate, d_upper


def token_grads(k, o, weights, cut):
    hidden, d_gate, d_upper = token_parts(k, o, weights, cut)
    return dot(k, d_gate, 0, 0), dot(k, d_upper, 0, 0), dot(hidden, o, 0, 0)


def cuts(width):
    _, half, quarter = place()
    return span(2 * half + 1 - quarter, width // 4), span(2 * half + quarter, width // 4)


def near_kernel(t0, t1, weights, send, keep, mine, keys, outer, sem):
    tokens, width = t0.shape[1:]
    piece = width // 4
    core, _, _ = place()
    copy = pltpu.make_async_copy(weights.at[core], mine, sem)
    copy.start()
    for at, src in enumerate((t0, t1)):
        keys[at * tokens : (at + 1) * tokens, :] = src[0]
        outer[at * tokens : (at + 1) * tokens, :] = src[1]
    copy.wait()
    for out, cut in zip((send, keep), cuts(width)):
        gate, upper, down = token_grads(keys[...], outer[...], mine, cut)
        out[0] = gate
        out[1] = upper
        for at in range(width // piece):
            out[2, at * piece : (at + 1) * piece, :] = down[:, at * piece : (at + 1) * piece]


def far_gate_kernel(t2, t3, mine, near_send, near_keep, send, keep, hidden, d_upper, keys, outer):
    tokens, width = t2.shape[1:]
    piece = width // 4
    for at, src in enumerate((t2, t3)):
        keys[at * tokens : (at + 1) * tokens, :] = src[0]
        outer[at * tokens : (at + 1) * tokens, :] = src[1]
    for at, (out, near, cut) in enumerate(zip((send, keep), (near_send, near_keep), cuts(width))):
        h, dg, du = token_parts(keys[...], outer[...], mine, cut)
        out[...] = (near[0] + dot(keys[...], dg, 0, 0)).astype(out.dtype)
        hidden[:, at * piece : (at + 1) * piece] = h
        d_upper[:, at * piece : (at + 1) * piece] = du


def far_rest_kernel(keys, outer, hidden, d_upper, near_send, near_keep, *outs):
    width = keys.shape[1]
    piece = width // 4
    for at, (out, near) in enumerate(zip((outs[:2], outs[2:]), (near_send, near_keep))):
        cut = slice(at * piece, (at + 1) * piece)
        out[0][...] = (near[1] + dot(keys[...], d_upper[:, cut], 0, 0)).astype(out[0].dtype)
        down = dot(hidden[:, cut], outer[...], 0, 0)
        for block in range(width // piece):
            rows = slice(block * piece, (block + 1) * piece)
            out[1][rows, :] = (near[2, rows, :] + down[:, rows]).astype(out[1].dtype)


def newton_schulz(matrix):
    wide = matrix.astype(F32)
    norm = jnp.sqrt(jnp.sum(wide * wide)) + 1e-07
    iterate = (wide * (1.0 / norm)).astype(BF16)
    half = matrix.shape[0] // 2
    for _ in range(NS_STEPS):
        upper = dot(iterate[:half], iterate, 1, 1).astype(BF16)
        corner = dot(iterate[half:], iterate[half:], 1, 1).astype(BF16)
        lower = jnp.concatenate([upper[:, half:].T, corner], axis=1)
        gram = jnp.concatenate([upper, lower], axis=0)
        mixed = (-4.775 * gram.astype(F32) + 2.0315 * dot(gram, gram)).astype(BF16)
        iterate = (3.4445 * iterate.astype(F32) + dot(mixed, iterate)).astype(BF16)
    return iterate


def renormed(old, update):
    old = old.astype(F32)
    fresh = old - update.astype(F32)
    scale = jnp.sqrt(
        (jnp.mean(old * old, axis=1, keepdims=True) + 1e-06)
        / (jnp.mean(fresh * fresh, axis=1, keepdims=True) + 1e-06)
    )
    return (fresh * scale).astype(BF16)


def ns_kernel(which, earlier, mine, *refs):
    count = len(which)
    pieces, (total, sems) = refs[: 4 * count], refs[-2:]
    if earlier:
        before, new, new_weights = refs[4 * count], *refs[-4:-2]
    else:
        new = refs[4 * count]
    _, width, _ = new.shape
    size = width // 4
    core, half, quarter = place()
    places = ((half, quarter), (half, 1 - quarter), (1 - half, quarter), (1 - half, 1 - quarter))
    for at, matrix in enumerate(which):
        for (h, q), piece in zip(places, pieces[4 * at : 4 * at + 4]):
            cut = span(2 * h + q, size)
            if matrix < 2:
                total[at, :, cut] = piece[...]
            else:
                for block in range(width // size):
                    rows = slice(block * size, (block + 1) * size)
                    total[at, cut, rows] = piece[rows, :]
    copies = []
    if earlier:
        for at, matrix in enumerate(earlier):
            copy = pltpu.make_async_copy(before.at[at], new_weights.at[core, matrix], sems.at[at])
            copy.start()
            copies.append(copy)
    updates = [newton_schulz(total[at]) for at in range(count)]
    for at, matrix in enumerate(which):
        new[at] = renormed(mine[matrix], updates[at])
    for copy in copies:
        copy.wait()


def updated(which, pieces, mine, earlier=(), before=None, held=None):
    heads, width = 2, mine.shape[2]
    count = len(which)
    flat = [piece for four in pieces for piece in four]
    out = [jax.ShapeDtypeStruct((count, width, width), BF16)]
    if earlier:
        flat.append(before)
        out.append(jax.ShapeDtypeStruct((heads, *mine.shape), BF16))
    specs = [VMEM_SPEC] * (len(flat) + 1)
    if held is not None:
        flat.append(held)
        specs.append(ANY_SPEC)
    return pl.pallas_call(
        functools.partial(ns_kernel, which, earlier),
        out_shape=out,
        in_specs=specs,
        input_output_aliases={} if held is None else {len(flat): 1},
        out_specs=[VMEM_SPEC, ANY_SPEC][: len(out)],
        scratch_shapes=[
            pltpu.VMEM((count, width, width), BF16),
            pltpu.SemaphoreType.DMA((max(1, len(earlier)),)),
        ],
        compiler_params=PARAMS,
        cost_estimate=pl.CostEstimate(
            flops=120 * NS_STEPS * count * width**3, bytes_accessed=64 * count * width**2, transcendentals=0
        ),
    )(mine, *flat)


def gate_up_kernel(queries, own, other, own_down, held, hidden, new_weights, readout, product, sems):
    width = own.shape[2]
    core, _, _ = place()
    copies = [
        pltpu.make_async_copy(other, new_weights.at[1 - core, pl.ds(0, 2)], sems.at[0]),
        pltpu.make_async_copy(own_down, new_weights.at[core, pl.ds(2, 1)], sems.at[1]),
        pltpu.make_async_copy(product, readout.at[:, span(core, width)], sems.at[2]),
    ]
    for copy in copies[:2]:
        copy.start()

    def units(head, part):
        cols = span(head, width)
        gate = dot(queries[:, cols], part[0])
        upper = dot(queries[:, cols], part[1])
        return (gate * jax.nn.sigmoid(gate) * upper).astype(BF16)

    product[...] = dot(units(core, own), own_down[0]).astype(BF16)
    copies[2].start()
    hidden[...] = units(1 - core, other)
    for copy in copies:
        copy.wait()


def down_kernel(hidden, other, held, held_readout, new_weights, readout, product, sems):
    width = other.shape[2]
    core, _, _ = place()
    copies = [
        pltpu.make_async_copy(other, new_weights.at[1 - core, pl.ds(2, 1)], sems.at[0]),
        pltpu.make_async_copy(product, readout.at[:, span(1 - core, width)], sems.at[1]),
    ]
    copies[0].start()
    product[...] = dot(hidden[...], other[0]).astype(BF16)
    copies[1].start()
    for copy in copies:
        copy.wait()


def body(size, keys, values, queries, rates, fast_weights):
    tokens = keys.shape[0]
    heads, _, width, _ = fast_weights.shape
    quarter = width // 4
    sibling = [(i, i ^ 1) for i in range(size)]
    first = [(i, i ^ (2 if i % 2 == 0 else 4)) for i in range(size)]
    second = [(i, i ^ (4 if i % 2 == 0 else 2)) for i in range(size)]
    across = [(i, i ^ 1 ^ (4 if i % 2 == 0 else 2)) for i in range(size)]
    rest = [[(i, i ^ (1 << bit)) for i in range(size)] for bit in range(3, size.bit_length() - 1)]

    def move(value, pairs):
        return lax.ppermute(value, "tok", pairs)

    def tie(*values):
        return lax.optimization_barrier(values)

    pair = jax.ShapeDtypeStruct((2, tokens, width), BF16)
    own, other = pl.pallas_call(
        pack_kernel,
        out_shape=(pair, pair),
        in_specs=[ANY_SPEC] * 3,
        out_specs=(VMEM_SPEC, VMEM_SPEC),
        scratch_shapes=[
            pltpu.VMEM(values.shape, BF16),
            pltpu.VMEM(rates.shape, F32),
            pltpu.SemaphoreType.DMA((4,)),
        ],
        compiler_params=WHOLE_VMEM,
    )(keys, values, rates)
    part16 = jax.ShapeDtypeStruct((width, quarter), BF16)
    part32 = jax.ShapeDtypeStruct((width, quarter), F32)
    three32 = jax.ShapeDtypeStruct((3, width, quarter), F32)
    rows_scratch = [pltpu.VMEM((2 * tokens, width), BF16)] * 2
    near_send, near_keep, mine = pl.pallas_call(
        near_kernel,
        out_shape=(three32, three32, jax.ShapeDtypeStruct((3, width, width), BF16)),
        in_specs=[VMEM_SPEC] * 2 + [ANY_SPEC],
        out_specs=(VMEM_SPEC,) * 3,
        scratch_shapes=rows_scratch + [pltpu.SemaphoreType.DMA],
        compiler_params=PARAMS,
    )(own, move(other, sibling), fast_weights)
    rows = jax.ShapeDtypeStruct((2 * tokens, width), BF16)
    units = jax.ShapeDtypeStruct((2 * tokens, width // 2), BF16)
    send_g, keep_g, hidden, d_upper, far_keys, far_outer = pl.pallas_call(
        far_gate_kernel,
        out_shape=(part16, part32, units, units, rows, rows),
        in_specs=[VMEM_SPEC] * 5,
        out_specs=(VMEM_SPEC,) * 6,
        compiler_params=PARAMS,
    )(move(own, first), move(other, across), mine, near_send, near_keep)
    send_u, send_d, keep_u, keep_d = pl.pallas_call(
        far_rest_kernel,
        out_shape=(part16,) * 2 + (part32,) * 2,
        in_specs=[VMEM_SPEC] * 6,
        out_specs=(VMEM_SPEC,) * 4,
        compiler_params=PARAMS,
        cost_estimate=pl.CostEstimate(flops=400 * tokens * width**2, bytes_accessed=64 * width**2, transcendentals=0),
    )(far_keys, far_outer, hidden, d_upper, near_send, near_keep)
    send, keep = (send_g, send_u, send_d), (keep_g, keep_u, keep_d)

    def reduced(at):
        return (keep[at] + move(send[at], second).astype(F32)).astype(BF16)

    def crossed(part):
        for pairs in rest:
            part = (part.astype(F32) + move(part, pairs).astype(F32)).astype(BF16)
        return part

    def pieces(part):
        over = move(part, second)
        return part, over, move(part, first), move(over, first)

    parts = [reduced(at) for at in range(3)]
    sums = [crossed(parts[0]), crossed(parts[1])]
    sums[0], parts[2] = tie(sums[0], parts[2])
    sums.append(crossed(parts[2]))
    four = [pieces(sums[0]), pieces(sums[1]), pieces(sums[2])]
    (new_a,) = updated((0, 1), four[:2], mine)
    new_d, new_weights = updated((2,), four[2:], mine, (0, 1), new_a)

    out_weights = jax.ShapeDtypeStruct(fast_weights.shape, BF16)
    out_readout = jax.ShapeDtypeStruct(queries.shape, BF16)
    half_readout = (tokens, width)
    hidden, new_weights, readout = pl.pallas_call(
        gate_up_kernel,
        out_shape=(jax.ShapeDtypeStruct(half_readout, BF16), out_weights, out_readout),
        in_specs=[VMEM_SPEC] * 4 + [ANY_SPEC],
        out_specs=(VMEM_SPEC, ANY_SPEC, ANY_SPEC),
        scratch_shapes=[pltpu.VMEM(half_readout, BF16), pltpu.SemaphoreType.DMA((3,))],
        input_output_aliases={4: 1},
        compiler_params=PARAMS,
    )(queries, new_a, move(new_a, sibling), new_d, new_weights)
    new_weights, readout = pl.pallas_call(
        down_kernel,
        out_shape=(out_weights, out_readout),
        in_specs=[VMEM_SPEC] * 2 + [ANY_SPEC] * 2,
        out_specs=(ANY_SPEC, ANY_SPEC),
        scratch_shapes=[pltpu.VMEM(half_readout, BF16), pltpu.SemaphoreType.DMA((2,))],
        input_output_aliases={2: 0, 3: 1},
        compiler_params=PARAMS,
    )(hidden, move(new_d, sibling), new_weights, readout)
    return readout, new_weights


def solution(mesh):
    return jax.shard_map(
        functools.partial(body, mesh.shape["tok"]),
        mesh=mesh,
        in_specs=(
            P(("grp", "tok"), None),
            P(("grp", "tok"), None),
            P(("grp", "tok"), None),
            P(None, ("grp", "tok")),
            P(),
        ),
        out_specs=(P(("grp", "tok"), None), P("grp", None, None, None)),
        check_vma=False,
    )
```

```python
import functools

import jax
import jax.numpy as jnp
from jax import lax
from jax.experimental import pallas as pl
from jax.experimental.pallas import tpu as pltpu
from jax.sharding import PartitionSpec as P

NS_STEPS = 2
F32 = jnp.float32
BF16 = jnp.bfloat16
VMEM_SPEC = pl.BlockSpec(memory_space=pltpu.VMEM)
ANY_SPEC = pl.BlockSpec(memory_space=pl.ANY)
PARAMS = pltpu.CompilerParams(vmem_limit_bytes=40 * 1024 * 1024)
WHOLE_VMEM = pltpu.CompilerParams(vmem_limit_bytes=62 * 1024 * 1024)


def place():
    me = lax.axis_index("tok")
    core = me % 2
    bit1 = (me // 2) % 2
    bit2 = (me // 4) % 2
    half = jnp.where(core == 0, bit1, bit2)
    quarter = jnp.where(core == 0, bit2, bit1)
    return core, half, quarter


def dot(a, b, ca=1, cb=0):
    return lax.dot_general(a, b, (((ca,), (cb,)), ((), ())), preferred_element_type=F32)


def span(at, size):
    return pl.ds(pl.multiple_of(at * size, size), size)


def pack_kernel(keys, values, rates, own, other, held, rate, sems):
    tokens, width = own.shape[1:]
    core, _, _ = place()
    copies = [
        pltpu.make_async_copy(values, held, sems.at[0]),
        pltpu.make_async_copy(rates, rate, sems.at[1]),
    ]
    for at, (head, out) in enumerate(((core, own), (1 - core, other))):
        copies.append(pltpu.make_async_copy(keys.at[:, span(head, width)], out.at[0], sems.at[2 + at]))
    for copy in copies:
        copy.start()
    for copy in copies[:2]:
        copy.wait()
    for head, out in ((core, own), (1 - core, other)):
        row = jnp.where(head == 0, rate[0:1, :], rate[1:2, :])
        column = jnp.broadcast_to(row, (tokens, tokens)).T[:, 0:1]
        out[1] = (-column * held[:, span(head, width)].astype(F32)).astype(BF16)
    for copy in copies[2:]:
        copy.wait()


def token_parts(k, o, weights, cut):
    gate = dot(k, weights[0, :, cut])
    upper = dot(k, weights[1, :, cut])
    back = dot(o, weights[2, cut, :], 1, 1)
    sigma = jax.nn.sigmoid(gate)
    silu_gate = gate * sigma
    hidden = (silu_gate * upper).astype(BF16)
    d_gate = (back * upper * sigma * (1.0 + gate * (1.0 - sigma))).astype(BF16)
    d_upper = (back * silu_gate).astype(BF16)
    return hidden, d_gate, d_upper


def token_grads(k, o, weights, cut):
    hidden, d_gate, d_upper = token_parts(k, o, weights, cut)
    return dot(k, d_gate, 0, 0), dot(k, d_upper, 0, 0), dot(hidden, o, 0, 0)


def cuts(width):
    _, half, quarter = place()
    return span(2 * half + 1 - quarter, width // 4), span(2 * half + quarter, width // 4)


def near_kernel(t0, t1, weights, send, keep, mine, keys, outer, sem):
    tokens, width = t0.shape[1:]
    piece = width // 4
    core, _, _ = place()
    copy = pltpu.make_async_copy(weights.at[core], mine, sem)
    copy.start()
    for at, src in enumerate((t0, t1)):
        keys[at * tokens : (at + 1) * tokens, :] = src[0]
        outer[at * tokens : (at + 1) * tokens, :] = src[1]
    copy.wait()
    for out, cut in zip((send, keep), cuts(width)):
        gate, upper, down = token_grads(keys[...], outer[...], mine, cut)
        out[0] = gate
        out[1] = upper
        for at in range(width // piece):
            out[2, at * piece : (at + 1) * piece, :] = down[:, at * piece : (at + 1) * piece]


def far_gate_kernel(t2, t3, mine, near_send, near_keep, send, keep, hidden, d_upper, keys, outer):
    tokens, width = t2.shape[1:]
    piece = width // 4
    for at, src in enumerate((t2, t3)):
        keys[at * tokens : (at + 1) * tokens, :] = src[0]
        outer[at * tokens : (at + 1) * tokens, :] = src[1]
    for at, (out, near, cut) in enumerate(zip((send, keep), (near_send, near_keep), cuts(width))):
        h, dg, du = token_parts(keys[...], outer[...], mine, cut)
        out[...] = (near[0] + dot(keys[...], dg, 0, 0)).astype(out.dtype)
        hidden[:, at * piece : (at + 1) * piece] = h
        d_upper[:, at * piece : (at + 1) * piece] = du


def far_rest_kernel(keys, outer, hidden, d_upper, near_send, near_keep, *outs):
    width = keys.shape[1]
    piece = width // 4
    for at, (out, near) in enumerate(zip((outs[:2], outs[2:]), (near_send, near_keep))):
        cut = slice(at * piece, (at + 1) * piece)
        out[0][...] = (near[1] + dot(keys[...], d_upper[:, cut], 0, 0)).astype(out[0].dtype)
        down = dot(hidden[:, cut], outer[...], 0, 0)
        for block in range(width // piece):
            rows = slice(block * piece, (block + 1) * piece)
            out[1][rows, :] = (near[2, rows, :] + down[:, rows]).astype(out[1].dtype)


def newton_schulz(matrix):
    wide = matrix.astype(F32)
    norm = jnp.sqrt(jnp.sum(wide * wide)) + 1e-07
    iterate = (wide * (1.0 / norm)).astype(BF16)
    half = matrix.shape[0] // 2
    for _ in range(NS_STEPS):
        upper = dot(iterate[:half], iterate, 1, 1).astype(BF16)
        corner = dot(iterate[half:], iterate[half:], 1, 1).astype(BF16)
        lower = jnp.concatenate([upper[:, half:].T, corner], axis=1)
        gram = jnp.concatenate([upper, lower], axis=0)
        mixed = (-4.775 * gram.astype(F32) + 2.0315 * dot(gram, gram)).astype(BF16)
        iterate = (3.4445 * iterate.astype(F32) + dot(mixed, iterate)).astype(BF16)
    return iterate


def renormed(old, update):
    old = old.astype(F32)
    fresh = old - update.astype(F32)
    scale = jnp.sqrt(
        (jnp.mean(old * old, axis=1, keepdims=True) + 1e-06)
        / (jnp.mean(fresh * fresh, axis=1, keepdims=True) + 1e-06)
    )
    return (fresh * scale).astype(BF16)


def ns_kernel(which, earlier, mine, *refs):
    count = len(which)
    pieces, (total, sems) = refs[: 4 * count], refs[-2:]
    if earlier:
        before, new, new_weights = refs[4 * count], *refs[-4:-2]
    else:
        new = refs[4 * count]
    _, width, _ = new.shape
    size = width // 4
    core, half, quarter = place()
    places = ((half, quarter), (half, 1 - quarter), (1 - half, quarter), (1 - half, 1 - quarter))
    for at, matrix in enumerate(which):
        for (h, q), piece in zip(places, pieces[4 * at : 4 * at + 4]):
            cut = span(2 * h + q, size)
            if matrix < 2:
                total[at, :, cut] = piece[...]
            else:
                for block in range(width // size):
                    rows = slice(block * size, (block + 1) * size)
                    total[at, cut, rows] = piece[rows, :]
    copies = []
    if earlier:
        for at, matrix in enumerate(earlier):
            copy = pltpu.make_async_copy(before.at[at], new_weights.at[core, matrix], sems.at[at])
            copy.start()
            copies.append(copy)
    updates = [newton_schulz(total[at]) for at in range(count)]
    for at, matrix in enumerate(which):
        new[at] = renormed(mine[matrix], updates[at])
    for copy in copies:
        copy.wait()


def updated(which, pieces, mine, earlier=(), before=None, held=None):
    heads, width = 2, mine.shape[2]
    count = len(which)
    flat = [piece for four in pieces for piece in four]
    out = [jax.ShapeDtypeStruct((count, width, width), BF16)]
    if earlier:
        flat.append(before)
        out.append(jax.ShapeDtypeStruct((heads, *mine.shape), BF16))
    specs = [VMEM_SPEC] * (len(flat) + 1)
    if held is not None:
        flat.append(held)
        specs.append(ANY_SPEC)
    return pl.pallas_call(
        functools.partial(ns_kernel, which, earlier),
        out_shape=out,
        in_specs=specs,
        input_output_aliases={} if held is None else {len(flat): 1},
        out_specs=[VMEM_SPEC, ANY_SPEC][: len(out)],
        scratch_shapes=[
            pltpu.VMEM((count, width, width), BF16),
            pltpu.SemaphoreType.DMA((max(1, len(earlier)),)),
        ],
        compiler_params=PARAMS,
        cost_estimate=pl.CostEstimate(
            flops=120 * NS_STEPS * count * width**3, bytes_accessed=64 * count * width**2, transcendentals=0
        ),
    )(mine, *flat)


def gate_up_kernel(queries, own, other, own_down, held, hidden, new_weights, readout, product, sems):
    width = own.shape[2]
    core, _, _ = place()
    copies = [
        pltpu.make_async_copy(other, new_weights.at[1 - core, pl.ds(0, 2)], sems.at[0]),
        pltpu.make_async_copy(own_down, new_weights.at[core, pl.ds(2, 1)], sems.at[1]),
        pltpu.make_async_copy(product, readout.at[:, span(core, width)], sems.at[2]),
    ]
    for copy in copies[:2]:
        copy.start()

    def units(head, part):
        cols = span(head, width)
        gate = dot(queries[:, cols], part[0])
        upper = dot(queries[:, cols], part[1])
        return (gate * jax.nn.sigmoid(gate) * upper).astype(BF16)

    product[...] = dot(units(core, own), own_down[0]).astype(BF16)
    copies[2].start()
    hidden[...] = units(1 - core, other)
    for copy in copies:
        copy.wait()


def down_kernel(hidden, other, held, held_readout, new_weights, readout, product, sems):
    width = other.shape[2]
    core, _, _ = place()
    copies = [
        pltpu.make_async_copy(other, new_weights.at[1 - core, pl.ds(2, 1)], sems.at[0]),
        pltpu.make_async_copy(product, readout.at[:, span(1 - core, width)], sems.at[1]),
    ]
    copies[0].start()
    product[...] = dot(hidden[...], other[0]).astype(BF16)
    copies[1].start()
    for copy in copies:
        copy.wait()


def body(size, keys, values, queries, rates, fast_weights):
    tokens = keys.shape[0]
    heads, _, width, _ = fast_weights.shape
    quarter = width // 4
    sibling = [(i, i ^ 1) for i in range(size)]
    first = [(i, i ^ (2 if i % 2 == 0 else 4)) for i in range(size)]
    second = [(i, i ^ (4 if i % 2 == 0 else 2)) for i in range(size)]
    across = [(i, i ^ 1 ^ (4 if i % 2 == 0 else 2)) for i in range(size)]
    rest = [[(i, i ^ (1 << bit)) for i in range(size)] for bit in range(3, size.bit_length() - 1)]

    def move(value, pairs):
        return lax.ppermute(value, "tok", pairs)

    def tie(*values):
        return lax.optimization_barrier(values)

    pair = jax.ShapeDtypeStruct((2, tokens, width), BF16)
    own, other = pl.pallas_call(
        pack_kernel,
        out_shape=(pair, pair),
        in_specs=[ANY_SPEC] * 3,
        out_specs=(VMEM_SPEC, VMEM_SPEC),
        scratch_shapes=[
            pltpu.VMEM(values.shape, BF16),
            pltpu.VMEM(rates.shape, F32),
            pltpu.SemaphoreType.DMA((4,)),
        ],
        compiler_params=WHOLE_VMEM,
    )(keys, values, rates)
    part16 = jax.ShapeDtypeStruct((width, quarter), BF16)
    part32 = jax.ShapeDtypeStruct((width, quarter), F32)
    three32 = jax.ShapeDtypeStruct((3, width, quarter), F32)
    rows_scratch = [pltpu.VMEM((2 * tokens, width), BF16)] * 2
    near_send, near_keep, mine = pl.pallas_call(
        near_kernel,
        out_shape=(three32, three32, jax.ShapeDtypeStruct((3, width, width), BF16)),
        in_specs=[VMEM_SPEC] * 2 + [ANY_SPEC],
        out_specs=(VMEM_SPEC,) * 3,
        scratch_shapes=rows_scratch + [pltpu.SemaphoreType.DMA],
        compiler_params=PARAMS,
    )(own, move(other, sibling), fast_weights)
    rows = jax.ShapeDtypeStruct((2 * tokens, width), BF16)
    units = jax.ShapeDtypeStruct((2 * tokens, width // 2), BF16)
    send_g, keep_g, hidden, d_upper, far_keys, far_outer = pl.pallas_call(
        far_gate_kernel,
        out_shape=(part16, part32, units, units, rows, rows),
        in_specs=[VMEM_SPEC] * 5,
        out_specs=(VMEM_SPEC,) * 6,
        compiler_params=PARAMS,
    )(move(own, first), move(other, across), mine, near_send, near_keep)
    send_u, send_d, keep_u, keep_d = pl.pallas_call(
        far_rest_kernel,
        out_shape=(part16,) * 2 + (part32,) * 2,
        in_specs=[VMEM_SPEC] * 6,
        out_specs=(VMEM_SPEC,) * 4,
        compiler_params=PARAMS,
        cost_estimate=pl.CostEstimate(flops=400 * tokens * width**2, bytes_accessed=64 * width**2, transcendentals=0),
    )(far_keys, far_outer, hidden, d_upper, near_send, near_keep)
    send, keep = (send_g, send_u, send_d), (keep_g, keep_u, keep_d)

    def reduced(at):
        return (keep[at] + move(send[at], second).astype(F32)).astype(BF16)

    def crossed(part):
        for pairs in rest:
            part = (part.astype(F32) + move(part, pairs).astype(F32)).astype(BF16)
        return part

    along_1 = [(i, i ^ 2) for i in range(size)]
    on_0 = place()[0] == 0

    def mixed(part):
        over_second, over_first = move(part, second), move(part, first)
        last = move(jnp.where(on_0, over_second, over_first), along_1)
        return part, over_second, over_first, last

    def pieces(part):
        over = move(part, second)
        return part, over, move(part, first), move(over, first)

    pair = move(jnp.stack(send[1:]), second)
    parts = [reduced(0)] + [(keep[1 + at] + pair[at].astype(F32)).astype(BF16) for at in range(2)]
    sums = [crossed(parts[0]), crossed(parts[1])]
    sums[0], parts[2] = tie(sums[0], parts[2])
    sums.append(crossed(parts[2]))
    four = [mixed(sums[0]), mixed(sums[1]), pieces(sums[2])]
    (new_a,) = updated((0, 1), four[:2], mine)
    new_d, new_weights = updated((2,), four[2:], mine, (0, 1), new_a)

    out_weights = jax.ShapeDtypeStruct(fast_weights.shape, BF16)
    out_readout = jax.ShapeDtypeStruct(queries.shape, BF16)
    half_readout = (tokens, width)
    hidden, new_weights, readout = pl.pallas_call(
        gate_up_kernel,
        out_shape=(jax.ShapeDtypeStruct(half_readout, BF16), out_weights, out_readout),
        in_specs=[VMEM_SPEC] * 4 + [ANY_SPEC],
        out_specs=(VMEM_SPEC, ANY_SPEC, ANY_SPEC),
        scratch_shapes=[pltpu.VMEM(half_readout, BF16), pltpu.SemaphoreType.DMA((3,))],
        input_output_aliases={4: 1},
        compiler_params=PARAMS,
    )(queries, new_a, move(new_a, sibling), new_d, new_weights)
    new_weights, readout = pl.pallas_call(
        down_kernel,
        out_shape=(out_weights, out_readout),
        in_specs=[VMEM_SPEC] * 2 + [ANY_SPEC] * 2,
        out_specs=(ANY_SPEC, ANY_SPEC),
        scratch_shapes=[pltpu.VMEM(half_readout, BF16), pltpu.SemaphoreType.DMA((2,))],
        input_output_aliases={2: 0, 3: 1},
        compiler_params=PARAMS,
    )(hidden, move(new_d, sibling), new_weights, readout)
    return readout, new_weights


def solution(mesh):
    return jax.shard_map(
        functools.partial(body, mesh.shape["tok"]),
        mesh=mesh,
        in_specs=(
            P(("grp", "tok"), None),
            P(("grp", "tok"), None),
            P(("grp", "tok"), None),
            P(None, ("grp", "tok")),
            P(),
        ),
        out_specs=(P(("grp", "tok"), None), P("grp", None, None, None)),
        check_vma=False,
    )
```

```python
import functools

import jax
import jax.numpy as jnp
from jax import lax
from jax.experimental import pallas as pl
from jax.experimental.pallas import tpu as pltpu
from jax.sharding import PartitionSpec as P

NS_STEPS = 2
F32 = jnp.float32
BF16 = jnp.bfloat16
VMEM_SPEC = pl.BlockSpec(memory_space=pltpu.VMEM)
ANY_SPEC = pl.BlockSpec(memory_space=pl.ANY)
PARAMS = pltpu.CompilerParams(vmem_limit_bytes=40 * 1024 * 1024)
WHOLE_VMEM = pltpu.CompilerParams(vmem_limit_bytes=62 * 1024 * 1024)


def place():
    me = lax.axis_index("tok")
    core = me % 2
    bit1 = (me // 2) % 2
    bit2 = (me // 4) % 2
    half = jnp.where(core == 0, bit1, bit2)
    quarter = jnp.where(core == 0, bit2, bit1)
    return core, half, quarter


def dot(a, b, ca=1, cb=0):
    return lax.dot_general(a, b, (((ca,), (cb,)), ((), ())), preferred_element_type=F32)


def span(at, size):
    return pl.ds(pl.multiple_of(at * size, size), size)


def pack_kernel(keys, values, rates, own, other, held, rate, sems):
    tokens, width = own.shape[1:]
    core, _, _ = place()
    copies = [
        pltpu.make_async_copy(values, held, sems.at[0]),
        pltpu.make_async_copy(rates, rate, sems.at[1]),
    ]
    for at, (head, out) in enumerate(((core, own), (1 - core, other))):
        copies.append(pltpu.make_async_copy(keys.at[:, span(head, width)], out.at[0], sems.at[2 + at]))
    for copy in copies:
        copy.start()
    for copy in copies[:2]:
        copy.wait()
    for head, out in ((core, own), (1 - core, other)):
        row = jnp.where(head == 0, rate[0:1, :], rate[1:2, :])
        column = jnp.broadcast_to(row, (tokens, tokens)).T[:, 0:1]
        out[1] = (-column * held[:, span(head, width)].astype(F32)).astype(BF16)
    for copy in copies[2:]:
        copy.wait()


def token_parts(k, o, weights, cut):
    gate = dot(k, weights[0, :, cut])
    upper = dot(k, weights[1, :, cut])
    back = dot(o, weights[2, cut, :], 1, 1)
    sigma = jax.nn.sigmoid(gate)
    silu_gate = gate * sigma
    hidden = (silu_gate * upper).astype(BF16)
    d_gate = (back * upper * sigma * (1.0 + gate * (1.0 - sigma))).astype(BF16)
    d_upper = (back * silu_gate).astype(BF16)
    return hidden, d_gate, d_upper


def token_grads(k, o, weights, cut):
    hidden, d_gate, d_upper = token_parts(k, o, weights, cut)
    return dot(k, d_gate, 0, 0), dot(k, d_upper, 0, 0), dot(hidden, o, 0, 0)


def cuts(width):
    _, half, quarter = place()
    yield span(2 * half + 1 - quarter, width // 4)
    yield span(2 * half + quarter, width // 4)


def near_kernel(t0, t1, weights, send, keep, mine, keys, outer, sem):
    tokens, width = t0.shape[1:]
    piece = width // 4
    core, _, _ = place()
    copy = pltpu.make_async_copy(weights.at[core], mine, sem)
    copy.start()
    for at, src in enumerate((t0, t1)):
        keys[at * tokens : (at + 1) * tokens, :] = src[0]
        outer[at * tokens : (at + 1) * tokens, :] = src[1]
    copy.wait()
    for out, cut in zip((send, keep), cuts(width)):
        gate, upper, down = token_grads(keys[...], outer[...], mine, cut)
        out[0] = gate
        out[1] = upper
        for at in range(width // piece):
            out[2, at * piece : (at + 1) * piece, :] = down[:, at * piece : (at + 1) * piece]


def far_gate_kernel(t2, t3, mine, near_send, send, hidden, d_upper, keys, outer):
    tokens, width = t2.shape[1:]
    for at, src in enumerate((t2, t3)):
        keys[at * tokens : (at + 1) * tokens, :] = src[0]
        outer[at * tokens : (at + 1) * tokens, :] = src[1]
    h, dg, du = token_parts(keys[...], outer[...], mine, next(cuts(width)))
    send[...] = (near_send[0] + dot(keys[...], dg, 0, 0)).astype(send.dtype)
    hidden[...] = h
    d_upper[...] = du


def far_rest_kernel(keys, outer, mine, hidden, d_upper, near_send, near_keep, send_u, send_d, keep_g, keep_u, keep_d):
    width = keys.shape[1]
    piece = width // 4
    _, cut = cuts(width)
    h, dg, du = token_parts(keys[...], outer[...], mine, cut)
    keep_g[...] = near_keep[0] + dot(keys[...], dg, 0, 0)
    for h, du, near, out_u, out_d in (
        (hidden[...], d_upper[...], near_send, send_u, send_d),
        (h, du, near_keep, keep_u, keep_d),
    ):
        out_u[...] = (near[1] + dot(keys[...], du, 0, 0)).astype(out_u.dtype)
        down = dot(h, outer[...], 0, 0)
        for block in range(width // piece):
            rows = slice(block * piece, (block + 1) * piece)
            out_d[rows, :] = (near[2, rows, :] + down[:, rows]).astype(out_d.dtype)


def newton_schulz(matrix):
    wide = matrix.astype(F32)
    norm = jnp.sqrt(jnp.sum(wide * wide)) + 1e-07
    iterate = (wide * (1.0 / norm)).astype(BF16)
    half = matrix.shape[0] // 2
    for _ in range(NS_STEPS):
        upper = dot(iterate[:half], iterate, 1, 1).astype(BF16)
        corner = dot(iterate[half:], iterate[half:], 1, 1).astype(BF16)
        lower = jnp.concatenate([upper[:, half:].T, corner], axis=1)
        gram = jnp.concatenate([upper, lower], axis=0)
        mixed = (-4.775 * gram.astype(F32) + 2.0315 * dot(gram, gram)).astype(BF16)
        iterate = (3.4445 * iterate.astype(F32) + dot(mixed, iterate)).astype(BF16)
    return iterate


def renormed(old, update):
    old = old.astype(F32)
    fresh = old - update.astype(F32)
    scale = jnp.sqrt(
        (jnp.mean(old * old, axis=1, keepdims=True) + 1e-06)
        / (jnp.mean(fresh * fresh, axis=1, keepdims=True) + 1e-06)
    )
    return (fresh * scale).astype(BF16)


def ns_kernel(which, earlier, mine, *refs):
    count = len(which)
    pieces, (total, sems) = refs[: 4 * count], refs[-2:]
    if earlier:
        before, new, new_weights = refs[4 * count], *refs[-4:-2]
    else:
        new = refs[4 * count]
    _, width, _ = new.shape
    size = width // 4
    core, half, quarter = place()
    places = ((half, quarter), (half, 1 - quarter), (1 - half, quarter), (1 - half, 1 - quarter))
    for at, matrix in enumerate(which):
        for (h, q), piece in zip(places, pieces[4 * at : 4 * at + 4]):
            cut = span(2 * h + q, size)
            if matrix < 2:
                total[at, :, cut] = piece[...]
            else:
                for block in range(width // size):
                    rows = slice(block * size, (block + 1) * size)
                    total[at, cut, rows] = piece[rows, :]
    copies = []
    if earlier:
        for at, matrix in enumerate(earlier):
            copy = pltpu.make_async_copy(before.at[at], new_weights.at[core, matrix], sems.at[at])
            copy.start()
            copies.append(copy)
    updates = [newton_schulz(total[at]) for at in range(count)]
    for at, matrix in enumerate(which):
        new[at] = renormed(mine[matrix], updates[at])
    for copy in copies:
        copy.wait()


def updated(which, pieces, mine, earlier=(), before=None, held=None):
    heads, width = 2, mine.shape[2]
    count = len(which)
    flat = [piece for four in pieces for piece in four]
    out = [jax.ShapeDtypeStruct((count, width, width), BF16)]
    if earlier:
        flat.append(before)
        out.append(jax.ShapeDtypeStruct((heads, *mine.shape), BF16))
    specs = [VMEM_SPEC] * (len(flat) + 1)
    if held is not None:
        flat.append(held)
        specs.append(ANY_SPEC)
    return pl.pallas_call(
        functools.partial(ns_kernel, which, earlier),
        out_shape=out,
        in_specs=specs,
        input_output_aliases={} if held is None else {len(flat): 1},
        out_specs=[VMEM_SPEC, ANY_SPEC][: len(out)],
        scratch_shapes=[
            pltpu.VMEM((count, width, width), BF16),
            pltpu.SemaphoreType.DMA((max(1, len(earlier)),)),
        ],
        compiler_params=PARAMS,
        cost_estimate=pl.CostEstimate(
            flops=120 * NS_STEPS * count * width**3, bytes_accessed=64 * count * width**2, transcendentals=0
        ),
    )(mine, *flat)


def gate_up_kernel(queries, own, other, own_down, held, hidden, new_weights, readout, product, sems):
    width = own.shape[2]
    core, _, _ = place()
    copies = [
        pltpu.make_async_copy(other, new_weights.at[1 - core, pl.ds(0, 2)], sems.at[0]),
        pltpu.make_async_copy(own_down, new_weights.at[core, pl.ds(2, 1)], sems.at[1]),
        pltpu.make_async_copy(product, readout.at[:, span(core, width)], sems.at[2]),
    ]
    for copy in copies[:2]:
        copy.start()

    def units(head, part):
        cols = span(head, width)
        gate = dot(queries[:, cols], part[0])
        upper = dot(queries[:, cols], part[1])
        return (gate * jax.nn.sigmoid(gate) * upper).astype(BF16)

    product[...] = dot(units(core, own), own_down[0]).astype(BF16)
    copies[2].start()
    hidden[...] = units(1 - core, other)
    for copy in copies:
        copy.wait()


def down_kernel(hidden, other, held, held_readout, new_weights, readout, product, sems):
    width = other.shape[2]
    core, _, _ = place()
    copies = [
        pltpu.make_async_copy(other, new_weights.at[1 - core, pl.ds(2, 1)], sems.at[0]),
        pltpu.make_async_copy(product, readout.at[:, span(1 - core, width)], sems.at[1]),
    ]
    copies[0].start()
    product[...] = dot(hidden[...], other[0]).astype(BF16)
    copies[1].start()
    for copy in copies:
        copy.wait()


def body(size, keys, values, queries, rates, fast_weights):
    tokens = keys.shape[0]
    heads, _, width, _ = fast_weights.shape
    quarter = width // 4
    sibling = [(i, i ^ 1) for i in range(size)]
    first = [(i, i ^ (2 if i % 2 == 0 else 4)) for i in range(size)]
    second = [(i, i ^ (4 if i % 2 == 0 else 2)) for i in range(size)]
    across = [(i, i ^ 1 ^ (4 if i % 2 == 0 else 2)) for i in range(size)]
    rest = [[(i, i ^ (1 << bit)) for i in range(size)] for bit in range(3, size.bit_length() - 1)]

    def move(value, pairs):
        return lax.ppermute(value, "tok", pairs)

    def tie(*values):
        return lax.optimization_barrier(values)

    pair = jax.ShapeDtypeStruct((2, tokens, width), BF16)
    own, other = pl.pallas_call(
        pack_kernel,
        out_shape=(pair, pair),
        in_specs=[ANY_SPEC] * 3,
        out_specs=(VMEM_SPEC, VMEM_SPEC),
        scratch_shapes=[
            pltpu.VMEM(values.shape, BF16),
            pltpu.VMEM(rates.shape, F32),
            pltpu.SemaphoreType.DMA((4,)),
        ],
        compiler_params=WHOLE_VMEM,
    )(keys, values, rates)
    part16 = jax.ShapeDtypeStruct((width, quarter), BF16)
    part32 = jax.ShapeDtypeStruct((width, quarter), F32)
    three32 = jax.ShapeDtypeStruct((3, width, quarter), F32)
    rows_scratch = [pltpu.VMEM((2 * tokens, width), BF16)] * 2
    near_send, near_keep, mine = pl.pallas_call(
        near_kernel,
        out_shape=(three32, three32, jax.ShapeDtypeStruct((3, width, width), BF16)),
        in_specs=[VMEM_SPEC] * 2 + [ANY_SPEC],
        out_specs=(VMEM_SPEC,) * 3,
        scratch_shapes=rows_scratch + [pltpu.SemaphoreType.DMA],
        compiler_params=PARAMS,
    )(own, move(other, sibling), fast_weights)
    rows = jax.ShapeDtypeStruct((2 * tokens, width), BF16)
    units = jax.ShapeDtypeStruct((2 * tokens, quarter), BF16)
    send_g, hidden, d_upper, far_keys, far_outer = pl.pallas_call(
        far_gate_kernel,
        out_shape=(part16, units, units, rows, rows),
        in_specs=[VMEM_SPEC] * 4,
        out_specs=(VMEM_SPEC,) * 5,
        compiler_params=PARAMS,
    )(move(own, first), move(other, across), mine, near_send)
    send_u, send_d, keep_g, keep_u, keep_d = pl.pallas_call(
        far_rest_kernel,
        out_shape=(part16,) * 2 + (part32,) * 3,
        in_specs=[VMEM_SPEC] * 7,
        out_specs=(VMEM_SPEC,) * 5,
        compiler_params=PARAMS,
        cost_estimate=pl.CostEstimate(flops=400 * tokens * width**2, bytes_accessed=64 * width**2, transcendentals=0),
    )(far_keys, far_outer, mine, hidden, d_upper, near_send, near_keep)
    send, keep = (send_g, send_u, send_d), (keep_g, keep_u, keep_d)

    def reduced(at):
        return (keep[at] + move(send[at], second).astype(F32)).astype(BF16)

    def crossed(part):
        for pairs in rest:
            part = (part.astype(F32) + move(part, pairs).astype(F32)).astype(BF16)
        return part

    along_1 = [(i, i ^ 2) for i in range(size)]
    on_0 = place()[0] == 0

    def mixed(part):
        over_second, over_first = move(part, second), move(part, first)
        last = move(jnp.where(on_0, over_second, over_first), along_1)
        return part, over_second, over_first, last

    def pieces(part):
        over = move(part, second)
        return part, over, move(part, first), move(over, first)

    pair = move(jnp.stack(send[1:]), second)
    parts = [reduced(0)] + [(keep[1 + at] + pair[at].astype(F32)).astype(BF16) for at in range(2)]
    sums = [crossed(parts[0]), crossed(parts[1])]
    sums[0], parts[2] = tie(sums[0], parts[2])
    sums.append(crossed(parts[2]))
    four = [mixed(sums[0]), mixed(sums[1]), pieces(sums[2])]
    (new_a,) = updated((0, 1), four[:2], mine)
    new_d, new_weights = updated((2,), four[2:], mine, (0, 1), new_a)

    out_weights = jax.ShapeDtypeStruct(fast_weights.shape, BF16)
    out_readout = jax.ShapeDtypeStruct(queries.shape, BF16)
    half_readout = (tokens, width)
    hidden, new_weights, readout = pl.pallas_call(
        gate_up_kernel,
        out_shape=(jax.ShapeDtypeStruct(half_readout, BF16), out_weights, out_readout),
        in_specs=[VMEM_SPEC] * 4 + [ANY_SPEC],
        out_specs=(VMEM_SPEC, ANY_SPEC, ANY_SPEC),
        scratch_shapes=[pltpu.VMEM(half_readout, BF16), pltpu.SemaphoreType.DMA((3,))],
        input_output_aliases={4: 1},
        compiler_params=PARAMS,
    )(queries, new_a, move(new_a, sibling), new_d, new_weights)
    new_weights, readout = pl.pallas_call(
        down_kernel,
        out_shape=(out_weights, out_readout),
        in_specs=[VMEM_SPEC] * 2 + [ANY_SPEC] * 2,
        out_specs=(ANY_SPEC, ANY_SPEC),
        scratch_shapes=[pltpu.VMEM(half_readout, BF16), pltpu.SemaphoreType.DMA((2,))],
        input_output_aliases={2: 0, 3: 1},
        compiler_params=PARAMS,
    )(hidden, move(new_d, sibling), new_weights, readout)
    return readout, new_weights


def solution(mesh):
    return jax.shard_map(
        functools.partial(body, mesh.shape["tok"]),
        mesh=mesh,
        in_specs=(
            P(("grp", "tok"), None),
            P(("grp", "tok"), None),
            P(("grp", "tok"), None),
            P(None, ("grp", "tok")),
            P(),
        ),
        out_specs=(P(("grp", "tok"), None), P("grp", None, None, None)),
        check_vma=False,
    )
```

```python
import functools

import jax
import jax.numpy as jnp
from jax import lax
from jax.experimental import pallas as pl
from jax.experimental.pallas import tpu as pltpu
from jax.sharding import PartitionSpec as P

NS_STEPS = 2
F32 = jnp.float32
BF16 = jnp.bfloat16
VMEM_SPEC = pl.BlockSpec(memory_space=pltpu.VMEM)
ANY_SPEC = pl.BlockSpec(memory_space=pl.ANY)
PARAMS = pltpu.CompilerParams(vmem_limit_bytes=40 * 1024 * 1024)
WHOLE_VMEM = pltpu.CompilerParams(vmem_limit_bytes=62 * 1024 * 1024)


def place():
    me = lax.axis_index("tok")
    core = me % 2
    bit1 = (me // 2) % 2
    bit2 = (me // 4) % 2
    half = jnp.where(core == 0, bit1, bit2)
    quarter = jnp.where(core == 0, bit2, bit1)
    return core, half, quarter


def dot(a, b, ca=1, cb=0):
    return lax.dot_general(a, b, (((ca,), (cb,)), ((), ())), preferred_element_type=F32)


def span(at, size):
    return pl.ds(pl.multiple_of(at * size, size), size)


def pack_kernel(keys, values, rates, own, other, held, rate, sems):
    tokens, width = own.shape[1:]
    core, _, _ = place()
    copies = [
        pltpu.make_async_copy(values, held, sems.at[0]),
        pltpu.make_async_copy(rates, rate, sems.at[1]),
    ]
    for at, (head, out) in enumerate(((core, own), (1 - core, other))):
        copies.append(pltpu.make_async_copy(keys.at[:, span(head, width)], out.at[0], sems.at[2 + at]))
    for copy in copies:
        copy.start()
    for copy in copies[:2]:
        copy.wait()
    for head, out in ((core, own), (1 - core, other)):
        row = jnp.where(head == 0, rate[0:1, :], rate[1:2, :])
        column = jnp.broadcast_to(row, (tokens, tokens)).T[:, 0:1]
        out[1] = (-column * held[:, span(head, width)].astype(F32)).astype(BF16)
    for copy in copies[2:]:
        copy.wait()


def token_parts(k, o, weights, cut):
    gate = dot(k, weights[0, :, cut])
    upper = dot(k, weights[1, :, cut])
    back = dot(o, weights[2, cut, :], 1, 1)
    sigma = jax.nn.sigmoid(gate)
    silu_gate = gate * sigma
    hidden = (silu_gate * upper).astype(BF16)
    d_gate = (back * upper * sigma * (1.0 + gate * (1.0 - sigma))).astype(BF16)
    d_upper = (back * silu_gate).astype(BF16)
    return hidden, d_gate, d_upper


def token_grads(k, o, weights, cut):
    hidden, d_gate, d_upper = token_parts(k, o, weights, cut)
    return dot(k, d_gate, 0, 0), dot(k, d_upper, 0, 0), dot(hidden, o, 0, 0)


def cuts(width):
    _, half, quarter = place()
    yield span(2 * half + 1 - quarter, width // 4)
    yield span(2 * half + quarter, width // 4)


def near_kernel(t0, t1, weights, send, keep, mine, keys, outer, sem):
    tokens, width = t0.shape[1:]
    piece = width // 4
    core, _, _ = place()
    copy = pltpu.make_async_copy(weights.at[core], mine, sem)
    copy.start()
    for at, src in enumerate((t0, t1)):
        keys[at * tokens : (at + 1) * tokens, :] = src[0]
        outer[at * tokens : (at + 1) * tokens, :] = src[1]
    copy.wait()
    for out, cut in zip((send, keep), cuts(width)):
        gate, upper, down = token_grads(keys[...], outer[...], mine, cut)
        out[0] = gate
        out[1] = upper
        for at in range(width // piece):
            out[2, at * piece : (at + 1) * piece, :] = down[:, at * piece : (at + 1) * piece]


def far_gate_kernel(t2, t3, mine, near_send, send, hidden, d_upper, keys, outer):
    tokens, width = t2.shape[1:]
    for at, src in enumerate((t2, t3)):
        keys[at * tokens : (at + 1) * tokens, :] = src[0]
        outer[at * tokens : (at + 1) * tokens, :] = src[1]
    h, dg, du = token_parts(keys[...], outer[...], mine, next(cuts(width)))
    send[...] = (near_send[0] + dot(keys[...], dg, 0, 0)).astype(send.dtype)
    hidden[...] = h
    d_upper[...] = du


def far_rest_kernel(keys, outer, mine, hidden, d_upper, near_send, near_keep, send_u, send_d, keep_g, keep_u, keep_d):
    width = keys.shape[1]
    piece = width // 4
    _, cut = cuts(width)
    h, dg, du = token_parts(keys[...], outer[...], mine, cut)
    keep_g[...] = near_keep[0] + dot(keys[...], dg, 0, 0)
    for h, du, near, out_u, out_d in (
        (hidden[...], d_upper[...], near_send, send_u, send_d),
        (h, du, near_keep, keep_u, keep_d),
    ):
        out_u[...] = (near[1] + dot(keys[...], du, 0, 0)).astype(out_u.dtype)
        down = dot(h, outer[...], 0, 0)
        for block in range(width // piece):
            rows = slice(block * piece, (block + 1) * piece)
            out_d[rows, :] = (near[2, rows, :] + down[:, rows]).astype(out_d.dtype)


def newton_schulz(matrix):
    wide = matrix.astype(F32)
    norm = jnp.sqrt(jnp.sum(wide * wide)) + 1e-07
    iterate = (wide * (1.0 / norm)).astype(BF16)
    half = matrix.shape[0] // 2
    for _ in range(NS_STEPS):
        upper = dot(iterate[:half], iterate, 1, 1).astype(BF16)
        corner = dot(iterate[half:], iterate[half:], 1, 1).astype(BF16)
        lower = jnp.concatenate([upper[:, half:].T, corner], axis=1)
        gram = jnp.concatenate([upper, lower], axis=0)
        mixed = (-4.775 * gram.astype(F32) + 2.0315 * dot(gram, gram)).astype(BF16)
        iterate = (3.4445 * iterate.astype(F32) + dot(mixed, iterate)).astype(BF16)
    return iterate


def renormed(old, update):
    old = old.astype(F32)
    fresh = old - update.astype(F32)
    scale = jnp.sqrt(
        (jnp.mean(old * old, axis=1, keepdims=True) + 1e-06)
        / (jnp.mean(fresh * fresh, axis=1, keepdims=True) + 1e-06)
    )
    return (fresh * scale).astype(BF16)


def ns_kernel(which, earlier, mine, *refs):
    count = len(which)
    pieces, (total, sems) = refs[: 4 * count], refs[-2:]
    if earlier:
        before, new, new_weights = refs[4 * count], *refs[-4:-2]
    else:
        new = refs[4 * count]
    _, width, _ = new.shape
    size = width // 4
    core, half, quarter = place()
    places = ((half, quarter), (half, 1 - quarter), (1 - half, quarter), (1 - half, 1 - quarter))
    for at, matrix in enumerate(which):
        for (h, q), piece in zip(places, pieces[4 * at : 4 * at + 4]):
            cut = span(2 * h + q, size)
            if matrix < 2:
                total[at, :, cut] = piece[...]
            else:
                for block in range(width // size):
                    rows = slice(block * size, (block + 1) * size)
                    total[at, cut, rows] = piece[rows, :]
    copies = []
    if earlier:
        for at, matrix in enumerate(earlier):
            copy = pltpu.make_async_copy(before.at[at], new_weights.at[core, matrix], sems.at[at])
            copy.start()
            copies.append(copy)
    updates = [newton_schulz(total[at]) for at in range(count)]
    for at, matrix in enumerate(which):
        new[at] = renormed(mine[matrix], updates[at])
    for copy in copies:
        copy.wait()


def updated(which, pieces, mine, earlier=(), before=None, held=None):
    heads, width = 2, mine.shape[2]
    count = len(which)
    flat = [piece for four in pieces for piece in four]
    out = [jax.ShapeDtypeStruct((count, width, width), BF16)]
    if earlier:
        flat.append(before)
        out.append(jax.ShapeDtypeStruct((heads, *mine.shape), BF16))
    specs = [VMEM_SPEC] * (len(flat) + 1)
    if held is not None:
        flat.append(held)
        specs.append(ANY_SPEC)
    return pl.pallas_call(
        functools.partial(ns_kernel, which, earlier),
        out_shape=out,
        in_specs=specs,
        input_output_aliases={} if held is None else {len(flat): 1},
        out_specs=[VMEM_SPEC, ANY_SPEC][: len(out)],
        scratch_shapes=[
            pltpu.VMEM((count, width, width), BF16),
            pltpu.SemaphoreType.DMA((max(1, len(earlier)),)),
        ],
        compiler_params=PARAMS,
        cost_estimate=pl.CostEstimate(
            flops=120 * NS_STEPS * count * width**3, bytes_accessed=64 * count * width**2, transcendentals=0
        ),
    )(mine, *flat)


def gate_up_kernel(queries, own, other, own_down, held, hidden, new_weights, readout, product, sems):
    width = own.shape[2]
    core, _, _ = place()
    copies = [
        pltpu.make_async_copy(other, new_weights.at[1 - core, pl.ds(0, 2)], sems.at[0]),
        pltpu.make_async_copy(own_down, new_weights.at[core, pl.ds(2, 1)], sems.at[1]),
        pltpu.make_async_copy(product, readout.at[:, span(core, width)], sems.at[2]),
    ]
    for copy in copies[:2]:
        copy.start()

    def units(head, part):
        cols = span(head, width)
        gate = dot(queries[:, cols], part[0])
        upper = dot(queries[:, cols], part[1])
        return (gate * jax.nn.sigmoid(gate) * upper).astype(BF16)

    product[...] = dot(units(core, own), own_down[0]).astype(BF16)
    copies[2].start()
    hidden[...] = units(1 - core, other)
    for copy in copies:
        copy.wait()


def down_kernel(hidden, other, held, held_readout, new_weights, readout, product, sems):
    width = other.shape[2]
    core, _, _ = place()
    copies = [
        pltpu.make_async_copy(other, new_weights.at[1 - core, pl.ds(2, 1)], sems.at[0]),
        pltpu.make_async_copy(product, readout.at[:, span(1 - core, width)], sems.at[1]),
    ]
    copies[0].start()
    product[...] = dot(hidden[...], other[0]).astype(BF16)
    copies[1].start()
    for copy in copies:
        copy.wait()


def body(size, keys, values, queries, rates, fast_weights):
    tokens = keys.shape[0]
    heads, _, width, _ = fast_weights.shape
    quarter = width // 4
    sibling = [(i, i ^ 1) for i in range(size)]
    first = [(i, i ^ (2 if i % 2 == 0 else 4)) for i in range(size)]
    second = [(i, i ^ (4 if i % 2 == 0 else 2)) for i in range(size)]
    across = [(i, i ^ 1 ^ (4 if i % 2 == 0 else 2)) for i in range(size)]
    rest = [[(i, i ^ (1 << bit)) for i in range(size)] for bit in range(3, size.bit_length() - 1)]

    def move(value, pairs):
        return lax.ppermute(value, "tok", pairs)

    def tie(*values):
        return lax.optimization_barrier(values)

    pair = jax.ShapeDtypeStruct((2, tokens, width), BF16)
    own, other = pl.pallas_call(
        pack_kernel,
        out_shape=(pair, pair),
        in_specs=[ANY_SPEC] * 3,
        out_specs=(VMEM_SPEC, VMEM_SPEC),
        scratch_shapes=[
            pltpu.VMEM(values.shape, BF16),
            pltpu.VMEM(rates.shape, F32),
            pltpu.SemaphoreType.DMA((4,)),
        ],
        compiler_params=WHOLE_VMEM,
    )(keys, values, rates)
    part16 = jax.ShapeDtypeStruct((width, quarter), BF16)
    part32 = jax.ShapeDtypeStruct((width, quarter), F32)
    three32 = jax.ShapeDtypeStruct((3, width, quarter), F32)
    rows_scratch = [pltpu.VMEM((2 * tokens, width), BF16)] * 2
    near_send, near_keep, mine = pl.pallas_call(
        near_kernel,
        out_shape=(three32, three32, jax.ShapeDtypeStruct((3, width, width), BF16)),
        in_specs=[VMEM_SPEC] * 2 + [ANY_SPEC],
        out_specs=(VMEM_SPEC,) * 3,
        scratch_shapes=rows_scratch + [pltpu.SemaphoreType.DMA],
        compiler_params=PARAMS,
    )(own, move(other, sibling), fast_weights)
    rows = jax.ShapeDtypeStruct((2 * tokens, width), BF16)
    units = jax.ShapeDtypeStruct((2 * tokens, quarter), BF16)
    send_g, hidden, d_upper, far_keys, far_outer = pl.pallas_call(
        far_gate_kernel,
        out_shape=(part16, units, units, rows, rows),
        in_specs=[VMEM_SPEC] * 4,
        out_specs=(VMEM_SPEC,) * 5,
        compiler_params=PARAMS,
    )(move(own, first), move(other, across), mine, near_send)
    send_u, send_d, keep_g, keep_u, keep_d = pl.pallas_call(
        far_rest_kernel,
        out_shape=(part16,) * 2 + (part32,) * 3,
        in_specs=[VMEM_SPEC] * 7,
        out_specs=(VMEM_SPEC,) * 5,
        compiler_params=PARAMS,
        cost_estimate=pl.CostEstimate(flops=400 * tokens * width**2, bytes_accessed=64 * width**2, transcendentals=0),
    )(far_keys, far_outer, mine, hidden, d_upper, near_send, near_keep)
    send, keep = (send_g, send_u, send_d), (keep_g, keep_u, keep_d)

    def reduced(at):
        return (keep[at] + move(send[at], second).astype(F32)).astype(BF16)

    def crossed(part):
        for pairs in rest:
            part = (part.astype(F32) + move(part, pairs).astype(F32)).astype(BF16)
        return part

    along_1 = [(i, i ^ 2) for i in range(size)]
    on_0 = place()[0] == 0

    def mixed(part):
        over_second, over_first = move(part, second), move(part, first)
        last = move(jnp.where(on_0, over_second, over_first), along_1)
        return part, over_second, over_first, last

    def pieces(part):
        over = move(part, second)
        return part, over, move(part, first), move(over, first)

    def paired(part):
        over = move(part, second)
        both = move(jnp.stack([part, over]), first)
        return part, over, both[0], both[1]

    pair = move(jnp.stack(send[1:]), second)
    parts = [reduced(0)] + [(keep[1 + at] + pair[at].astype(F32)).astype(BF16) for at in range(2)]
    sums = [crossed(parts[0]), crossed(parts[1])]
    sums[0], parts[2] = tie(sums[0], parts[2])
    sums.append(crossed(parts[2]))
    four = [mixed(sums[0]), mixed(sums[1]), paired(sums[2])]
    (new_a,) = updated((0, 1), four[:2], mine)
    new_d, new_weights = updated((2,), four[2:], mine, (0, 1), new_a)

    out_weights = jax.ShapeDtypeStruct(fast_weights.shape, BF16)
    out_readout = jax.ShapeDtypeStruct(queries.shape, BF16)
    half_readout = (tokens, width)
    hidden, new_weights, readout = pl.pallas_call(
        gate_up_kernel,
        out_shape=(jax.ShapeDtypeStruct(half_readout, BF16), out_weights, out_readout),
        in_specs=[VMEM_SPEC] * 4 + [ANY_SPEC],
        out_specs=(VMEM_SPEC, ANY_SPEC, ANY_SPEC),
        scratch_shapes=[pltpu.VMEM(half_readout, BF16), pltpu.SemaphoreType.DMA((3,))],
        input_output_aliases={4: 1},
        compiler_params=PARAMS,
    )(queries, new_a, move(new_a, sibling), new_d, new_weights)
    new_weights, readout = pl.pallas_call(
        down_kernel,
        out_shape=(out_weights, out_readout),
        in_specs=[VMEM_SPEC] * 2 + [ANY_SPEC] * 2,
        out_specs=(ANY_SPEC, ANY_SPEC),
        scratch_shapes=[pltpu.VMEM(half_readout, BF16), pltpu.SemaphoreType.DMA((2,))],
        input_output_aliases={2: 0, 3: 1},
        compiler_params=PARAMS,
    )(hidden, move(new_d, sibling), new_weights, readout)
    return readout, new_weights


def solution(mesh):
    return jax.shard_map(
        functools.partial(body, mesh.shape["tok"]),
        mesh=mesh,
        in_specs=(
            P(("grp", "tok"), None),
            P(("grp", "tok"), None),
            P(("grp", "tok"), None),
            P(None, ("grp", "tok")),
            P(),
        ),
        out_specs=(P(("grp", "tok"), None), P("grp", None, None, None)),
        check_vma=False,
    )
```

```python
import functools

import jax
import jax.numpy as jnp
from jax import lax
from jax.experimental import pallas as pl
from jax.experimental.pallas import tpu as pltpu
from jax.sharding import PartitionSpec as P

NS_STEPS = 2
F32 = jnp.float32
BF16 = jnp.bfloat16
VMEM_SPEC = pl.BlockSpec(memory_space=pltpu.VMEM)
ANY_SPEC = pl.BlockSpec(memory_space=pl.ANY)
PARAMS = pltpu.CompilerParams(vmem_limit_bytes=40 * 1024 * 1024)
WHOLE_VMEM = pltpu.CompilerParams(vmem_limit_bytes=62 * 1024 * 1024)


def place():
    me = lax.axis_index("tok")
    core = me % 2
    bit1 = (me // 2) % 2
    bit2 = (me // 4) % 2
    half = jnp.where(core == 0, bit1, bit2)
    quarter = jnp.where(core == 0, bit2, bit1)
    return core, half, quarter


def dot(a, b, ca=1, cb=0):
    return lax.dot_general(a, b, (((ca,), (cb,)), ((), ())), preferred_element_type=F32)


def span(at, size):
    return pl.ds(pl.multiple_of(at * size, size), size)


def pack_kernel(keys, values, rates, own, other, held, rate, sems):
    tokens, width = own.shape[1:]
    core, _, _ = place()
    copies = [
        pltpu.make_async_copy(values, held, sems.at[0]),
        pltpu.make_async_copy(rates, rate, sems.at[1]),
    ]
    for at, (head, out) in enumerate(((core, own), (1 - core, other))):
        copies.append(pltpu.make_async_copy(keys.at[:, span(head, width)], out.at[0], sems.at[2 + at]))
    for copy in copies:
        copy.start()
    for copy in copies[:2]:
        copy.wait()
    for head, out in ((core, own), (1 - core, other)):
        row = jnp.where(head == 0, rate[0:1, :], rate[1:2, :])
        column = jnp.broadcast_to(row, (tokens, tokens)).T[:, 0:1]
        out[1] = (-column * held[:, span(head, width)].astype(F32)).astype(BF16)
    for copy in copies[2:]:
        copy.wait()


def token_parts(k, o, weights, cut):
    gate = dot(k, weights[0, :, cut])
    upper = dot(k, weights[1, :, cut])
    back = dot(o, weights[2, cut, :], 1, 1)
    sigma = jax.nn.sigmoid(gate)
    silu_gate = gate * sigma
    hidden = (silu_gate * upper).astype(BF16)
    d_gate = (back * upper * sigma * (1.0 + gate * (1.0 - sigma))).astype(BF16)
    d_upper = (back * silu_gate).astype(BF16)
    return hidden, d_gate, d_upper


def token_grads(k, o, weights, cut):
    hidden, d_gate, d_upper = token_parts(k, o, weights, cut)
    return dot(k, d_gate, 0, 0), dot(k, d_upper, 0, 0), dot(hidden, o, 0, 0)


def cuts(width):
    _, half, quarter = place()
    yield span(2 * half + 1 - quarter, width // 4)
    yield span(2 * half + quarter, width // 4)


def near_kernel(t0, t1, weights, send, keep, mine, keys, outer, sem):
    tokens, width = t0.shape[1:]
    piece = width // 4
    core, _, _ = place()
    copy = pltpu.make_async_copy(weights.at[core], mine, sem)
    copy.start()
    for at, src in enumerate((t0, t1)):
        keys[at * tokens : (at + 1) * tokens, :] = src[0]
        outer[at * tokens : (at + 1) * tokens, :] = src[1]
    copy.wait()
    for out, cut in zip((send, keep), cuts(width)):
        gate, upper, down = token_grads(keys[...], outer[...], mine, cut)
        out[0] = gate
        out[1] = upper
        for at in range(width // piece):
            out[2, at * piece : (at + 1) * piece, :] = down[:, at * piece : (at + 1) * piece]


def far_gate_kernel(t2, t3, mine, near_send, send, hidden, d_upper, keys, outer):
    tokens, width = t2.shape[1:]
    for at, src in enumerate((t2, t3)):
        keys[at * tokens : (at + 1) * tokens, :] = src[0]
        outer[at * tokens : (at + 1) * tokens, :] = src[1]
    h, dg, du = token_parts(keys[...], outer[...], mine, next(cuts(width)))
    send[...] = (near_send[0] + dot(keys[...], dg, 0, 0)).astype(send.dtype)
    hidden[...] = h
    d_upper[...] = du


def far_rest_kernel(keys, outer, mine, hidden, d_upper, near_send, near_keep, send_u, send_d, keep_g, keep_u, keep_d):
    width = keys.shape[1]
    piece = width // 4
    _, cut = cuts(width)
    h, dg, du = token_parts(keys[...], outer[...], mine, cut)
    keep_g[...] = near_keep[0] + dot(keys[...], dg, 0, 0)
    for h, du, near, out_u, out_d in (
        (hidden[...], d_upper[...], near_send, send_u, send_d),
        (h, du, near_keep, keep_u, keep_d),
    ):
        out_u[...] = (near[1] + dot(keys[...], du, 0, 0)).astype(out_u.dtype)
        down = dot(h, outer[...], 0, 0)
        for block in range(width // piece):
            rows = slice(block * piece, (block + 1) * piece)
            out_d[rows, :] = (near[2, rows, :] + down[:, rows]).astype(out_d.dtype)


def newton_schulz(matrix):
    wide = matrix.astype(F32)
    norm = jnp.sqrt(jnp.sum(wide * wide)) + 1e-07
    iterate = (wide * (1.0 / norm)).astype(BF16)
    half = matrix.shape[0] // 2
    for _ in range(NS_STEPS):
        upper = dot(iterate[:half], iterate, 1, 1).astype(BF16)
        corner = dot(iterate[half:], iterate[half:], 1, 1).astype(BF16)
        lower = jnp.concatenate([upper[:, half:].T, corner], axis=1)
        gram = jnp.concatenate([upper, lower], axis=0)
        mixed = (-4.775 * gram.astype(F32) + 2.0315 * dot(gram, gram)).astype(BF16)
        iterate = (3.4445 * iterate.astype(F32) + dot(mixed, iterate)).astype(BF16)
    return iterate


def renormed(old, update):
    old = old.astype(F32)
    fresh = old - update.astype(F32)
    scale = jnp.sqrt(
        (jnp.mean(old * old, axis=1, keepdims=True) + 1e-06)
        / (jnp.mean(fresh * fresh, axis=1, keepdims=True) + 1e-06)
    )
    return (fresh * scale).astype(BF16)


def ns_kernel(which, earlier, mine, *refs):
    count = len(which)
    pieces, (total, sems) = refs[: 4 * count], refs[-2:]
    if earlier:
        before, new, new_weights = refs[4 * count], *refs[-4:-2]
    else:
        new = refs[4 * count]
    _, width, _ = new.shape
    size = width // 4
    core, half, quarter = place()
    places = ((half, quarter), (half, 1 - quarter), (1 - half, quarter), (1 - half, 1 - quarter))
    for at, matrix in enumerate(which):
        for (h, q), piece in zip(places, pieces[4 * at : 4 * at + 4]):
            cut = span(2 * h + q, size)
            if matrix < 2:
                total[at, :, cut] = piece[...]
            else:
                for block in range(width // size):
                    rows = slice(block * size, (block + 1) * size)
                    total[at, cut, rows] = piece[rows, :]
    copies = []
    if earlier:
        for at, matrix in enumerate(earlier):
            copy = pltpu.make_async_copy(before.at[at], new_weights.at[core, matrix], sems.at[at])
            copy.start()
            copies.append(copy)
    updates = [newton_schulz(total[at]) for at in range(count)]
    for at, matrix in enumerate(which):
        new[at] = renormed(mine[matrix], updates[at])
    for copy in copies:
        copy.wait()


def updated(which, pieces, mine, earlier=(), before=None, held=None):
    heads, width = 2, mine.shape[2]
    count = len(which)
    flat = [piece for four in pieces for piece in four]
    out = [jax.ShapeDtypeStruct((count, width, width), BF16)]
    if earlier:
        flat.append(before)
        out.append(jax.ShapeDtypeStruct((heads, *mine.shape), BF16))
    specs = [VMEM_SPEC] * (len(flat) + 1)
    if held is not None:
        flat.append(held)
        specs.append(ANY_SPEC)
    return pl.pallas_call(
        functools.partial(ns_kernel, which, earlier),
        out_shape=out,
        in_specs=specs,
        input_output_aliases={} if held is None else {len(flat): 1},
        out_specs=[VMEM_SPEC, ANY_SPEC][: len(out)],
        scratch_shapes=[
            pltpu.VMEM((count, width, width), BF16),
            pltpu.SemaphoreType.DMA((max(1, len(earlier)),)),
        ],
        compiler_params=PARAMS,
        cost_estimate=pl.CostEstimate(
            flops=120 * NS_STEPS * count * width**3, bytes_accessed=64 * count * width**2, transcendentals=0
        ),
    )(mine, *flat)


def gate_up_kernel(queries, own, other, own_down, held, hidden, new_weights, readout, product, sems):
    width = own.shape[2]
    core, _, _ = place()
    copies = [
        pltpu.make_async_copy(other, new_weights.at[1 - core, pl.ds(0, 2)], sems.at[0]),
        pltpu.make_async_copy(product, readout.at[:, span(core, width)], sems.at[1]),
    ]
    copies[0].start()

    def units(head, part):
        cols = span(head, width)
        gate = dot(queries[:, cols], part[0])
        upper = dot(queries[:, cols], part[1])
        return (gate * jax.nn.sigmoid(gate) * upper).astype(BF16)

    product[...] = dot(units(core, own), own_down[0]).astype(BF16)
    copies[1].start()
    hidden[...] = units(1 - core, other)
    for copy in copies:
        copy.wait()


def down_kernel(hidden, own, other, held, held_readout, new_weights, readout, product, sems):
    width = other.shape[2]
    core, _, _ = place()
    copies = [
        pltpu.make_async_copy(other, new_weights.at[1 - core, pl.ds(2, 1)], sems.at[0]),
        pltpu.make_async_copy(own, new_weights.at[core, pl.ds(2, 1)], sems.at[1]),
        pltpu.make_async_copy(product, readout.at[:, span(1 - core, width)], sems.at[2]),
    ]
    for copy in copies[:2]:
        copy.start()
    product[...] = dot(hidden[...], other[0]).astype(BF16)
    copies[2].start()
    for copy in copies:
        copy.wait()


def body(size, keys, values, queries, rates, fast_weights):
    tokens = keys.shape[0]
    heads, _, width, _ = fast_weights.shape
    quarter = width // 4
    sibling = [(i, i ^ 1) for i in range(size)]
    first = [(i, i ^ (2 if i % 2 == 0 else 4)) for i in range(size)]
    second = [(i, i ^ (4 if i % 2 == 0 else 2)) for i in range(size)]
    across = [(i, i ^ 1 ^ (4 if i % 2 == 0 else 2)) for i in range(size)]
    rest = [[(i, i ^ (1 << bit)) for i in range(size)] for bit in range(3, size.bit_length() - 1)]

    def move(value, pairs):
        return lax.ppermute(value, "tok", pairs)

    def tie(*values):
        return lax.optimization_barrier(values)

    pair = jax.ShapeDtypeStruct((2, tokens, width), BF16)
    own, other = pl.pallas_call(
        pack_kernel,
        out_shape=(pair, pair),
        in_specs=[ANY_SPEC] * 3,
        out_specs=(VMEM_SPEC, VMEM_SPEC),
        scratch_shapes=[
            pltpu.VMEM(values.shape, BF16),
            pltpu.VMEM(rates.shape, F32),
            pltpu.SemaphoreType.DMA((4,)),
        ],
        compiler_params=WHOLE_VMEM,
    )(keys, values, rates)
    part16 = jax.ShapeDtypeStruct((width, quarter), BF16)
    part32 = jax.ShapeDtypeStruct((width, quarter), F32)
    three32 = jax.ShapeDtypeStruct((3, width, quarter), F32)
    rows_scratch = [pltpu.VMEM((2 * tokens, width), BF16)] * 2
    near_send, near_keep, mine = pl.pallas_call(
        near_kernel,
        out_shape=(three32, three32, jax.ShapeDtypeStruct((3, width, width), BF16)),
        in_specs=[VMEM_SPEC] * 2 + [ANY_SPEC],
        out_specs=(VMEM_SPEC,) * 3,
        scratch_shapes=rows_scratch + [pltpu.SemaphoreType.DMA],
        compiler_params=PARAMS,
    )(own, move(other, sibling), fast_weights)
    rows = jax.ShapeDtypeStruct((2 * tokens, width), BF16)
    units = jax.ShapeDtypeStruct((2 * tokens, quarter), BF16)
    send_g, hidden, d_upper, far_keys, far_outer = pl.pallas_call(
        far_gate_kernel,
        out_shape=(part16, units, units, rows, rows),
        in_specs=[VMEM_SPEC] * 4,
        out_specs=(VMEM_SPEC,) * 5,
        compiler_params=PARAMS,
    )(move(own, first), move(other, across), mine, near_send)
    send_u, send_d, keep_g, keep_u, keep_d = pl.pallas_call(
        far_rest_kernel,
        out_shape=(part16,) * 2 + (part32,) * 3,
        in_specs=[VMEM_SPEC] * 7,
        out_specs=(VMEM_SPEC,) * 5,
        compiler_params=PARAMS,
        cost_estimate=pl.CostEstimate(flops=400 * tokens * width**2, bytes_accessed=64 * width**2, transcendentals=0),
    )(far_keys, far_outer, mine, hidden, d_upper, near_send, near_keep)
    send, keep = (send_g, send_u, send_d), (keep_g, keep_u, keep_d)

    def reduced(at):
        return (keep[at] + move(send[at], second).astype(F32)).astype(BF16)

    def crossed(part):
        for pairs in rest:
            part = (part.astype(F32) + move(part, pairs).astype(F32)).astype(BF16)
        return part

    along_1 = [(i, i ^ 2) for i in range(size)]
    on_0 = place()[0] == 0

    def mixed(part):
        over_second, over_first = move(part, second), move(part, first)
        last = move(jnp.where(on_0, over_second, over_first), along_1)
        return part, over_second, over_first, last

    def pieces(part):
        over = move(part, second)
        return part, over, move(part, first), move(over, first)

    pair = move(jnp.stack(send[1:]), second)
    parts = [reduced(0)] + [(keep[1 + at] + pair[at].astype(F32)).astype(BF16) for at in range(2)]
    sums = [crossed(parts[0]), crossed(parts[1])]
    sums[0], parts[2] = tie(sums[0], parts[2])
    sums.append(crossed(parts[2]))
    four = [mixed(sums[0]), mixed(sums[1]), pieces(sums[2])]
    (new_a,) = updated((0, 1), four[:2], mine)
    new_d, new_weights = updated((2,), four[2:], mine, (0, 1), new_a)

    out_weights = jax.ShapeDtypeStruct(fast_weights.shape, BF16)
    out_readout = jax.ShapeDtypeStruct(queries.shape, BF16)
    half_readout = (tokens, width)
    hidden, new_weights, readout = pl.pallas_call(
        gate_up_kernel,
        out_shape=(jax.ShapeDtypeStruct(half_readout, BF16), out_weights, out_readout),
        in_specs=[VMEM_SPEC] * 4 + [ANY_SPEC],
        out_specs=(VMEM_SPEC, ANY_SPEC, ANY_SPEC),
        scratch_shapes=[pltpu.VMEM(half_readout, BF16), pltpu.SemaphoreType.DMA((2,))],
        input_output_aliases={4: 1},
        compiler_params=PARAMS,
    )(queries, new_a, move(new_a, sibling), new_d, new_weights)
    new_weights, readout = pl.pallas_call(
        down_kernel,
        out_shape=(out_weights, out_readout),
        in_specs=[VMEM_SPEC] * 3 + [ANY_SPEC] * 2,
        out_specs=(ANY_SPEC, ANY_SPEC),
        scratch_shapes=[pltpu.VMEM(half_readout, BF16), pltpu.SemaphoreType.DMA((3,))],
        input_output_aliases={3: 0, 4: 1},
        compiler_params=PARAMS,
    )(hidden, new_d, move(new_d, sibling), new_weights, readout)
    return readout, new_weights


def solution(mesh):
    return jax.shard_map(
        functools.partial(body, mesh.shape["tok"]),
        mesh=mesh,
        in_specs=(
            P(("grp", "tok"), None),
            P(("grp", "tok"), None),
            P(("grp", "tok"), None),
            P(None, ("grp", "tok")),
            P(),
        ),
        out_specs=(P(("grp", "tok"), None), P("grp", None, None, None)),
        check_vma=False,
    )
```
